512 devices in a mesh: dp: 8 (over z), vocab: 64 (over y, x, core).
Axes of the slice: x: 4, y: 8, z: 8, core: 2. Of those that a mesh axis runs over, the one named last changes fastest.
Arguments:
- hidden: bfloat16 [384, 7168], P(None, 'dp'), may hold values from -150 to 150
- tokens: int32 [384], replicated, may hold values from 0 to 65535
- final_gain: float32 [7168], P('dp'), may hold values from 0.25 to 1.75
- hidden_gain: float32 [7168], P('dp'), may hold values from 0.25 to 1.75
- embed_gain: float32 [7168], P('dp'), may hold values from 0.25 to 1.75
- embed_table: bfloat16 [65536, 7168], P('vocab', 'dp'), may hold values from -150 to 150
- proj_hidden: bfloat16 [7168, 7168], P('dp', 'vocab'), may hold values from -0.046875 to 0.046875
- proj_embed: bfloat16 [7168, 7168], P('dp', 'vocab'), may hold values from -0.046875 to 0.046875
- draft_gain: float32 [7168], P('vocab'), may hold values from 0.25 to 1.75
- head_weight: bfloat16 [7168, 65536], P('dp', 'vocab'), may hold values from -6.1419227 to 6.1419227
Outputs:
- main_logp: bfloat16 [384, 65536], P('dp', 'vocab')
- draft_logp: bfloat16 [384, 65536], P('dp', 'vocab')
The draws below stay inside these ranges and needn't reach their ends.
All inputs are finite; a program needn't handle non-finite values.
Results may differ from the reference program's by a relative error of at most 0.0047.
Values may be sent and summed in bfloat16 or wider, within the bound.
No kernel may reach another device: no remote copies, remote signals or barrier semaphores. Data moves between devices by JAX's collectives and lax.ppermute only.
A program may use at most 64 MiB of HBM per device.

```python
import math
import jax
import jax.numpy as jnp
from jax import lax

D = 7168
ROWS = 384
V = 65536


def feature_ramp(steep):
    return jnp.sqrt(1.0 + steep * jnp.arange(D, dtype=jnp.float32) / D)


def draw_hidden(key, part):
    key = jax.random.fold_in(key, 1)
    first, second = jax.random.split(key)
    base = jnp.clip(jax.random.normal(first, (ROWS, D), jnp.float32), -5.0, 5.0)
    scales = jnp.exp(jax.random.uniform(second, (ROWS, 1), jnp.float32, 0.0, math.log(4.0)))
    ramp = feature_ramp(2.0)
    return (base * scales * ramp).astype(jnp.bfloat16)


def draw_embed_table(key, part):
    key = jax.random.fold_in(key, 2)
    first, second = jax.random.split(key)
    base = jnp.clip(jax.random.normal(first, (V, D), jnp.float32), -5.0, 5.0)
    scales = jnp.exp(jax.random.uniform(second, (V, 1), jnp.float32, 0.0, math.log(2.0)))
    ramp = feature_ramp(2.0)
    return (base * scales * ramp).astype(jnp.bfloat16)


def draw_head_weight(key, part):
    key = jax.random.fold_in(key, 3)
    first, second = jax.random.split(key, 2)
    base = jnp.clip(jax.random.normal(first, (D, V), jnp.float32), -5.0, 5.0)
    spread = jnp.exp(jax.random.uniform(second, (1, V), jnp.float32, 0.0, math.log(10.0)))
    weight = base * spread / math.sqrt(D)
    return weight.astype(jnp.bfloat16)


def plant(values, own_key, low, high):
    longest = values.shape.index(max(values.shape))
    spots = []
    for shift in (0, 1):
        where = [jax.random.randint(jax.random.fold_in(own_key, axis), (), 0, length) for axis, length in enumerate(values.shape)]
        where[longest] = (where[longest] + shift) % values.shape[longest]
        spots.append(tuple(where))
    return values.at[spots[0]].set(low).at[spots[1]].set(high)


def level_of(rng, shape, cuts, least, top_value):
    factor_of = 1.0
    for dim, parts in cuts:
        steps = jax.random.uniform(jax.random.fold_in(jax.random.fold_in(rng, 6), dim), (parts,), jnp.float32, least / len(cuts), top_value / len(cuts))
        factor_of = factor_of * jnp.repeat(jnp.exp(steps), shape[dim] // parts).reshape((-1,) + (1,) * (len(shape) - 1 - dim))
    return factor_of


def normal_values(stream_key, shape, scale, reach, shards=(), held_as=jnp.bfloat16):
    result = scale * jax.random.normal(stream_key, shape, jnp.float32)
    if shards:
        result = result * level_of(stream_key, shape, shards, -0.22, 0.18)
    return jnp.clip(result, -reach, reach).astype(held_as)


def setup_inputs(seed: int = 0) -> dict:
    streams_of = jax.random.split(jax.random.key(seed), 11)
    hidden = draw_hidden(jax.random.fold_in(streams_of[10], 71), 0)
    tokens = plant(jax.random.randint(streams_of[1], (ROWS,), 0, V), jax.random.fold_in(streams_of[1], 1), 0, V - 1).astype(jnp.int32)
    final_gain = jnp.clip(1.0 + 0.15 * jax.random.normal(streams_of[2], (D,), jnp.float32), 0.25, 1.75)
    hidden_gain = jnp.clip(1.0 + 0.15 * jax.random.normal(streams_of[3], (D,), jnp.float32), 0.25, 1.75)
    embed_gain = jnp.clip(1.0 + 0.15 * jax.random.normal(streams_of[4], (D,), jnp.float32), 0.25, 1.75)
    embed_table = draw_embed_table(jax.random.fold_in(streams_of[10], 71), 0)
    proj_hidden = normal_values(streams_of[6], (D, D), (2 * D) ** -0.5, 0.046875, ((0, 8), (1, 64)))
    proj_embed = normal_values(streams_of[7], (D, D), (2 * D) ** -0.5, 0.046875, ((0, 8), (1, 64)))
    draft_gain = jnp.clip(1.0 + 0.15 * jax.random.normal(streams_of[8], (D,), jnp.float32), 0.25, 1.75)
    head_weight = draw_head_weight(jax.random.fold_in(streams_of[10], 71), 0)
    return dict(hidden=hidden, tokens=tokens, final_gain=final_gain, hidden_gain=hidden_gain, embed_gain=embed_gain, embed_table=embed_table, proj_hidden=proj_hidden, proj_embed=proj_embed, draft_gain=draft_gain, head_weight=head_weight)


def rms_scale(values):
    return lax.rsqrt(lax.optimization_barrier(jnp.mean(values * values, axis=1, keepdims=True)) + 1e-06)

def log_probs(logits):
    top = lax.optimization_barrier(jnp.max(logits, axis=1, keepdims=True))
    total = lax.optimization_barrier(jnp.sum(jnp.exp(logits - top), axis=1, keepdims=True))
    return (logits - top - jnp.log(total)).astype(jnp.bfloat16)

def reference(hidden, tokens, final_gain, hidden_gain, embed_gain, embed_table, proj_hidden, proj_embed, draft_gain, head_weight):
    hidden_f = hidden.astype(jnp.float32)
    inv_hidden = rms_scale(hidden_f)
    main_normed = (hidden_f * inv_hidden * final_gain).astype(jnp.bfloat16)
    main_logp = log_probs(jnp.dot(main_normed, head_weight, preferred_element_type=jnp.float32))
    embedded = jnp.take(embed_table, tokens.astype(jnp.int32), axis=0).astype(jnp.float32)
    inv_embed = rms_scale(embedded)
    joined_hidden = (hidden_f * inv_hidden * hidden_gain).astype(jnp.bfloat16)
    joined_embed = (embedded * inv_embed * embed_gain).astype(jnp.bfloat16)
    projected = jnp.dot(joined_hidden, proj_hidden, preferred_element_type=jnp.float32) + jnp.dot(joined_embed, proj_embed, preferred_element_type=jnp.float32)
    draft_normed = (projected * rms_scale(projected) * draft_gain).astype(jnp.bfloat16)
    draft_logp = log_probs(jnp.dot(draft_normed, head_weight, preferred_element_type=jnp.float32))
    return (main_logp, draft_logp)
```

```python
import functools

import jax
import jax.numpy as jnp
from jax import lax
from jax.experimental import pallas as pl
from jax.experimental.pallas import tpu as pltpu
from jax.sharding import PartitionSpec as P

EPS = 1e-06
BF, F32 = jnp.bfloat16, jnp.float32
ROWS, D, V = 384, 7168, 65536
NZ, NY, NX, NC = 8, 8, 4, 2
FD = D // NZ
VD = V // (NY * NX * NC)
CW = D // (NY * NX * NC)
RB = ROWS // NZ
UR = RB // (NX * NC)
L = 128
WROWS = 2 * FD + 16
ZROWS = 2 * RB + 16
HROWS = RB * (VD // L) + 8
PARAMS = pltpu.CompilerParams(vmem_limit_bytes=48 * 1024 * 1024)


def vid(y, x, c):
    return (y * NX + x) * NC + c


CORE = [[vid(y, x, c) for c in range(NC)] for y in range(NY) for x in range(NX)]
YS = [[vid(y, x, c) for y in range(NY)] for x in range(NX) for c in range(NC)]
XY = [[vid(y, x, c) for y in range(NY) for x in range(NX)] for c in range(NC)]
XC = [[vid(y, x, c) for x in range(NX) for c in range(NC)] for y in range(NY)]


def iota(shape, dim):
    return lax.broadcasted_iota(jnp.int32, shape, dim)


def split(x):
    hi = x.astype(BF).astype(F32)
    return hi, x - hi


def call(kernel, outs, *args):
    single = not isinstance(outs, (list, tuple))
    shapes = [outs] if single else list(outs)
    specs = [pl.BlockSpec(memory_space=pltpu.VMEM) for _ in shapes]
    return pl.pallas_call(
        kernel,
        out_shape=shapes[0] if single else shapes,
        in_specs=[pl.BlockSpec(memory_space=pltpu.VMEM)] * len(args),
        out_specs=specs[0] if single else specs,
        compiler_params=PARAMS,
    )(*args)


def struct(shape, dtype):
    return jax.ShapeDtypeStruct(shape, dtype)


def pack_kernel(ph, pe, gain, out):
    out[:, CW:] = jnp.zeros((WROWS, L - CW), BF)
    out[0:FD, 0:CW] = ph[...]
    out[FD : 2 * FD, 0:CW] = pe[...]
    hi, rest = split(gain[...])
    mid, low = split(rest)
    row = iota((16, CW), 0)
    out[2 * FD :, 0:CW] = jnp.where(row == 0, hi, jnp.where(row == 1, mid, jnp.where(row == 2, low, 0.0))).astype(BF)


def pick_kernel(tokens, table, out):
    base = lax.axis_index("vocab") * VD
    units = NY * NX
    rows = NC * units * 8
    tok = tokens[...]
    part = iota((8, ROWS), 0)
    high = jnp.broadcast_to(tok >> 8, (8, ROWS)).astype(F32)
    low = jnp.broadcast_to(tok & 255, (8, ROWS)).astype(F32)
    codes = jnp.where(part == 0, high, jnp.where(part == 1, low, 0.0)).astype(BF)
    pos = iota((rows, ROWS), 0)
    step, unit, core = pos & 7, (pos >> 3) & (units - 1), pos >> 8
    source = (unit * NC + core) * UR + step
    select = ((iota((rows, ROWS), 1) == source) & (step < UR)).astype(F32).astype(BF)
    found = lax.dot_general(select, codes, (((1,), (1,)), ((), ())), preferred_element_type=F32)
    local = (found[:, 0:1] * 256.0 + found[:, 1:2]).astype(jnp.int32) - base
    local = jnp.where((iota((rows, 1), 0) & 7) < UR, local, -1)
    for start in range(0, rows, 128):
        hot = (iota((128, VD), 1) == local[start : start + 128]).astype(F32).astype(BF)
        out[start : start + 128, :] = jnp.dot(hot, table[...], preferred_element_type=F32).astype(BF)


def proj_kernel(picked, hidden, hidden_gain, embed_gain, weights, out):
    y = lax.axis_index("vocab") // (NX * NC)
    h = hidden[pl.ds(pl.multiple_of(y * RB, 16), RB), :].astype(F32)
    row, col = iota((RB, 64), 0), iota((RB, 64), 1)
    source = (row // UR) * 8 + row % UR
    select = (col == source).astype(F32).astype(BF)
    e = jnp.dot(select, picked[...], preferred_element_type=F32)
    lane = iota((RB, L), 1)

    def extra(x):
        hi, low = split(jnp.sum(x * x, axis=1, keepdims=True))
        return jnp.where(lane == CW, hi, jnp.where(lane == CW + 1, low, 0.0))

    extra_h, extra_e = extra(h), extra(e)
    hg = (h * hidden_gain[...]).astype(BF)
    eg = (e * embed_gain[...]).astype(BF)
    for t in range(NY):
        out[t, 0:RB, :] = (jnp.dot(hg, weights[t, 0:FD, :], preferred_element_type=F32) + extra_h).astype(BF)
        out[t, RB : 2 * RB, :] = (
            jnp.dot(eg, weights[t, FD : 2 * FD, :], preferred_element_type=F32) + extra_e
        ).astype(BF)
        out[t, 2 * RB :, :] = weights[t, 2 * FD :, :]


def join_kernel(parts, out):
    total = parts[0].astype(F32)
    gain = jnp.sum(total[2 * RB :, :], axis=0, keepdims=True)
    for k in range(1, NZ):
        total = total + parts[k].astype(F32)
    lane = iota((RB, L), 1)
    sides = (lane == CW) | (lane == CW + 1)

    def scale(x):
        return lax.rsqrt(jnp.sum(jnp.where(sides, x, 0.0), axis=1, keepdims=True) / D + EPS)

    h, e = total[0:RB], total[RB : 2 * RB]
    inv_h = scale(h)
    projected = jnp.where(lane < CW, h * inv_h + e * scale(e), 0.0)
    sq_hi, sq_low = split(jnp.sum(projected * projected, axis=1, keepdims=True))
    h_hi, h_low = split(inv_h)
    x = projected * gain
    for k, v in enumerate((sq_hi, sq_low, h_hi, h_low)):
        x = jnp.where(lane == CW + k, v, x)
    out[...] = jnp.broadcast_to(x.astype(BF)[None], out.shape)


def head_kernel(rows, head, out, x_ref):
    squares = jnp.zeros((ROWS, L), F32)
    for x in range(NX):
        for c in range(NC):
            a = jnp.concatenate([rows[c, y * NX + x] for y in range(NY)], axis=0)
            j = x * NC + c
            x_ref[:, j * CW : (j + 1) * CW] = a[:, 0:CW]
            squares = squares + a.astype(F32)
            if j == 0:
                scales = a.astype(F32)
    lane = iota((ROWS, L), 1)
    sq = jnp.sum(jnp.where((lane == CW) | (lane == CW + 1), squares, 0.0), axis=1, keepdims=True)
    inv_h = jnp.sum(jnp.where((lane == CW + 2) | (lane == CW + 3), scales, 0.0), axis=1, keepdims=True)
    diagonal = iota((RB, L), 0) == iota((RB, L), 1)
    part = iota((8, L), 0)
    for k in range(NZ):
        tail = jnp.zeros((8, L), F32)
        for n, col in enumerate((sq, inv_h)):
            line = jnp.sum(jnp.where(diagonal, col[k * RB : (k + 1) * RB], 0.0), axis=0, keepdims=True)
            hi, low = split(line)
            tail = jnp.where(part == 2 * n, hi, jnp.where(part == 2 * n + 1, low, tail))
        out[k, HROWS - 8 :, :] = tail.astype(BF)
    for n in range(0, VD, 256):
        acc = jnp.dot(x_ref[...], head[:, n : n + 256], preferred_element_type=F32).astype(BF)
        for m in range(2):
            tile = n // L + m
            for k in range(NZ):
                out[k, tile * RB : (tile + 1) * RB, :] = acc[k * RB : (k + 1) * RB, m * L : (m + 1) * L]


def stats_kernel(parts, main, main_out, draft_out, stats):
    diagonal = iota((RB, L), 0) == iota((RB, L), 1)

    def column(line):
        return jnp.sum(jnp.where(diagonal, line, 0.0), axis=1, keepdims=True)

    def line(col):
        return jnp.sum(jnp.where(diagonal, col, 0.0), axis=0, keepdims=True)

    tail = parts[0, HROWS - 8 :, :].astype(F32)
    inv_h = column(tail[2:3] + tail[3:4])
    for k in range(1, NZ):
        tail = tail + parts[k, HROWS - 8 :, :].astype(F32)
    inv_d = lax.rsqrt(column(tail[0:1] + tail[1:2]) / D + EPS)
    main_logits = main[...] * inv_h
    main_out[...] = main_logits
    for t in range(VD // L):
        acc = parts[0, t * RB : (t + 1) * RB, :].astype(F32)
        for k in range(1, NZ):
            acc = acc + parts[k, t * RB : (t + 1) * RB, :].astype(F32)
        draft_out[:, t * L : (t + 1) * L] = acc * inv_d
    draft_logits = draft_out[...]
    part = iota((8, L), 0)
    value = jnp.zeros((8, L), F32)
    for n, logits in enumerate((main_logits, draft_logits)):
        top = jnp.max(logits, axis=1, keepdims=True)
        total = jnp.sum(jnp.exp(logits - top), axis=1, keepdims=True)
        value = jnp.where(part == 2 * n, line(top), jnp.where(part == 2 * n + 1, line(total), value))
    stats[...] = jnp.broadcast_to(value[None], stats.shape)


def final_kernel(stats, main, draft, main_out, draft_out):
    diagonal = iota((RB, L), 0) == iota((RB, L), 1)
    every = stats[...]
    for n, (logits, out) in enumerate(((main, main_out), (draft, draft_out))):
        tops, sums = every[:, 2 * n, :], every[:, 2 * n + 1, :]
        top = jnp.max(tops, axis=0, keepdims=True)
        total = jnp.sum(sums * jnp.exp(tops - top), axis=0, keepdims=True)
        top_col = jnp.sum(jnp.where(diagonal, top, 0.0), axis=1, keepdims=True)
        log_col = jnp.log(jnp.sum(jnp.where(diagonal, total, 0.0), axis=1, keepdims=True))
        out[...] = (logits[...] - top_col - log_col).astype(BF)


def exchange(x, groups):
    return lax.all_to_all(x, "vocab", 0, 0, axis_index_groups=groups)


def per_device(
    hidden,
    tokens,
    final_gain,
    hidden_gain,
    embed_gain,
    embed_table,
    proj_hidden,
    proj_embed,
    draft_gain,
    head_weight,
):
    packed = call(pack_kernel, struct((WROWS, L), BF), proj_hidden, proj_embed, draft_gain[None])
    weights = lax.all_gather(packed, "vocab", axis_index_groups=YS)

    picked = call(pick_kernel, struct((NC * NY * NX * 8, FD), BF), tokens[None], embed_table)
    half = exchange(picked.reshape(NC, NY * NX, 8, FD), CORE)
    half = half[0] + half[1]
    unit = jnp.sum(exchange(half, XY).astype(F32), axis=0).astype(BF)
    mine = exchange(jnp.broadcast_to(unit[None], (NX * NC, 8, FD)), XC).reshape(NX * NC * 8, FD)

    main_in = (hidden.astype(F32) * final_gain).astype(BF)
    main_part = jnp.dot(main_in, head_weight, preferred_element_type=F32)
    main = lax.psum_scatter(main_part, "dp", scatter_dimension=0, tiled=True)

    partial = call(
        proj_kernel, struct((NY, ZROWS, L), BF), mine, hidden, hidden_gain[None], embed_gain[None], weights
    )
    joined = call(join_kernel, struct((NY * NX, RB, L), BF), lax.all_to_all(partial, "dp", 0, 0))
    rows = lax.all_gather(exchange(joined, XY), "vocab", axis_index_groups=CORE)
    blocks = pl.pallas_call(
        head_kernel,
        out_shape=struct((NZ, HROWS, L), BF),
        in_specs=[pl.BlockSpec(memory_space=pltpu.VMEM)] * 2,
        out_specs=pl.BlockSpec(memory_space=pltpu.VMEM),
        scratch_shapes=[pltpu.VMEM((ROWS, FD), BF)],
        compiler_params=PARAMS,
    )(rows, head_weight)
    parts = lax.all_to_all(blocks, "dp", 0, 0)
    main_logits, draft_logits, stats = call(
        stats_kernel,
        (struct((RB, VD), F32), struct((RB, VD), F32), struct((NY * NX * NC, 8, L), F32)),
        parts,
        main,
    )
    stats = lax.all_to_all(stats, "vocab", 0, 0)
    main_logp, draft_logp = call(
        final_kernel, (struct((RB, VD), BF), struct((RB, VD), BF)), stats, main_logits, draft_logits
    )
    return (main_logp, draft_logp)


def solution(mesh):
    return jax.shard_map(
        per_device,
        mesh=mesh,
        in_specs=(
            P(None, "dp"),
            P(),
            P("dp"),
            P("dp"),
            P("dp"),
            P("vocab", "dp"),
            P("dp", "vocab"),
            P("dp", "vocab"),
            P("vocab"),
            P("dp", "vocab"),
        ),
        out_specs=(P("dp", "vocab"), P("dp", "vocab")),
        check_vma=False,
    )
```

```python
import jax
import jax.numpy as jnp
from jax import lax
from jax.experimental import pallas as pl
from jax.experimental.pallas import tpu as pltpu
from jax.sharding import PartitionSpec as P

EPS = 1e-06
BF, F32 = jnp.bfloat16, jnp.float32
ROWS, D, V = 384, 7168, 65536
NZ, NY, NX, NC = 8, 8, 4, 2
NQ = NY * NX
FD = D // NZ
VD = V // (NQ * NC)
CW = D // (NQ * NC)
RB = ROWS // NZ
UR = ROWS // (NQ * NC)
PAIR = 2 * CW // NQ
L = 128
TILES = VD // L
ZR = NX * 8 + 16
HR = 2 * RB * TILES + 16
PARAMS = pltpu.CompilerParams(vmem_limit_bytes=48 * 1024 * 1024)


def vid(y, x, c):
    return (y * NX + x) * NC + c


CORE = [[vid(y, x, c) for c in range(NC)] for y in range(NY) for x in range(NX)]
XY = [[vid(y, x, c) for y in range(NY) for x in range(NX)] for c in range(NC)]


def iota(shape, dim):
    return lax.broadcasted_iota(jnp.int32, shape, dim)


def split(x):
    hi = x.astype(BF).astype(F32)
    return hi, x - hi


def ones(mask):
    return mask.astype(F32).astype(BF)


def dot(a, b):
    return jnp.dot(a, b, preferred_element_type=F32)


def dot_nt(a, b):
    return lax.dot_general(a, b, (((1,), (1,)), ((), ())), preferred_element_type=F32)


def dot_tn(a, b):
    return lax.dot_general(a, b, (((0,), (0,)), ((), ())), preferred_element_type=F32)


def line(col):
    same = iota((L, L), 0) == iota((L, L), 1)
    parts = [
        jnp.sum(jnp.where(same, col[k : k + L], 0.0), axis=0, keepdims=True) for k in range(0, col.shape[0], L)
    ]
    return jnp.concatenate(parts, axis=1)


def place(rows, shape):
    row = iota(shape, 0)
    out = jnp.zeros(shape, F32)
    for k, v in enumerate(rows):
        out = jnp.where(row == k, v, out)
    return out


def call(kernel, outs, *args, scratch=()):
    single = not isinstance(outs, (list, tuple))
    shapes = [outs] if single else list(outs)
    specs = [pl.BlockSpec(memory_space=pltpu.VMEM) for _ in shapes]
    return pl.pallas_call(
        kernel,
        out_shape=shapes[0] if single else shapes,
        in_specs=[pl.BlockSpec(memory_space=pltpu.VMEM)] * len(args),
        out_specs=specs[0] if single else specs,
        scratch_shapes=list(scratch),
        compiler_params=PARAMS,
    )(*args)


def struct(shape, dtype):
    return jax.ShapeDtypeStruct(shape, dtype)


def pick_kernel(tokens, table, out):
    base = lax.axis_index("vocab") * VD
    rows = NC * NQ * 8
    tok = tokens[...]
    part = iota((8, ROWS), 0)
    high = jnp.broadcast_to(tok >> 8, (8, ROWS)).astype(F32)
    low = jnp.broadcast_to(tok & 255, (8, ROWS)).astype(F32)
    codes = jnp.where(part == 0, high, jnp.where(part == 1, low, 0.0)).astype(BF)
    pos = iota((rows, ROWS), 0)
    step, unit, core = pos & 7, (pos >> 3) & (NQ - 1), pos >> 8
    source = (unit * NC + core) * UR + step
    found = dot_nt(ones((iota((rows, ROWS), 1) == source) & (step < UR)), codes)
    local = (found[:, 0:1] * 256.0 + found[:, 1:2]).astype(jnp.int32) - base
    local = jnp.where((iota((rows, 1), 0) & 7) < UR, local, -1)
    for start in range(0, rows, L):
        hot = ones(iota((L, VD), 1) == local[start : start + L])
        out[start : start + L, :] = dot(hot, table[...]).astype(BF)


def share_kernel(ph, pe, out):
    rows = NQ * 8
    both = jnp.concatenate([ph[...], pe[...]], axis=0)
    pos = iota((rows, 2 * CW), 0)
    unit, k, side = pos >> 3, pos & 3, (pos >> 2) & 1
    source = side * CW + (unit >> 1) * PAIR + (unit & 1) * 4 + k
    valid = k < 4 - (unit & 1)
    out[...] = dot(ones((iota((rows, 2 * CW), 1) == source) & valid), both).astype(BF)


def send_kernel(half, share, out):
    for k in range(NQ):
        rows = half[0, k].astype(F32) + half[1, k].astype(F32)
        out[k] = jnp.concatenate([rows, share[k].astype(F32)], axis=0).astype(BF)


def unit_kernel(got, gain, rows, weights):
    total = jnp.zeros((8, FD), F32)
    for k in range(NQ):
        block = got[k].astype(F32)
        total = total + block[0:8]
        weights[k] = block[8:16].astype(BF)
    hi, rest = split(gain[...])
    mid, low = split(rest)
    spare = jnp.concatenate([hi, mid, low, jnp.zeros((1, FD - 3 * L), F32)], axis=1)
    total = jnp.where(iota((8, FD), 0) == UR, spare, total)
    rows[...] = jnp.broadcast_to(total.astype(BF)[None], rows.shape)


def main_kernel(hidden, gain, head, out, squares):
    h = hidden[...].astype(F32)
    squares[...] = place([line(jnp.sum(h * h, axis=1, keepdims=True))], (8, ROWS))
    x = (h * gain[...]).astype(BF)
    for n in range(0, VD, 256):
        acc = dot(x, head[:, n : n + 256]).astype(BF)
        for m in range(2):
            t = n // L + m
            for k in range(NZ):
                out[k, t * RB : (t + 1) * RB, :] = acc[k * RB : (k + 1) * RB, m * L : (m + 1) * L]


def proj_kernel(picked, hidden, hidden_gain, embed_gain, weights, squares, out):
    pos, row = iota((ROWS, NC * NQ * 8), 1), iota((ROWS, NC * NQ * 8), 0)
    step, unit, core = pos & 7, (pos >> 3) & (NQ - 1), pos >> 8
    select = ones((row == (unit * NC + core) * UR + step) & (step < UR))
    e = dot(select, picked[...])
    e_sq = line(jnp.sum(e * e, axis=1, keepdims=True))
    hg = (hidden[...].astype(F32) * hidden_gain[...]).astype(BF)
    eg = (e * embed_gain[...]).astype(BF)
    w = weights[...]
    both = jnp.where((iota((NQ * 8, ROWS), 0) & 4) == 0, dot_nt(w, hg), dot_nt(w, eg)).astype(BF)
    tail = place([*split(squares[0:1, :]), *split(e_sq)], (16, ROWS)).astype(BF)
    for t in range(NY):
        out[t, 0 : NX * 8, :] = both[t * NX * 8 : (t + 1) * NX * 8]
        out[t, NX * 8 :, :] = tail


def join_kernel(parts, out):
    total = parts[0].astype(F32)
    for k in range(1, NZ):
        total = total + parts[k].astype(F32)
    n = NX * 8
    inv_h = lax.rsqrt((total[n : n + 1] + total[n + 1 : n + 2]) / D + EPS)
    inv_e = lax.rsqrt((total[n + 2 : n + 3] + total[n + 3 : n + 4]) / D + EPS)
    body = total[0:n]
    row = iota((16, n), 0)
    first = (row >> 2) * 8 + (row & 3)
    pick_h = (iota((16, n), 1) == first).astype(F32)
    pick_e = (iota((16, n), 1) == first + 4).astype(F32)
    exact = lax.Precision.HIGHEST
    joined = inv_h * jnp.dot(pick_h, body, precision=exact) + inv_e * jnp.dot(pick_e, body, precision=exact)
    out[...] = jnp.broadcast_to(joined.astype(BF)[None], out.shape)


def gained_kernel(picked, head, out, scaled):
    z = lax.axis_index("dp")
    same = iota((CW, L), 0) == iota((CW, L), 1)
    for x in range(NX):
        for c in range(NC):
            start = pl.multiple_of((c * NQ + z * NX + x // 2 * 2) * 8, 16)
            at = x % 2 * 8 + UR
            unit = picked[pl.ds(start, 16), :].astype(F32)[at : at + 1]
            gain = unit[:, 0:L] + unit[:, L : 2 * L] + unit[:, 2 * L : 3 * L]
            col = jnp.sum(jnp.where(same, gain, 0.0), axis=1, keepdims=True)
            j = (x * NC + c) * CW
            scaled[j : j + CW, :] = (head[j : j + CW, :].astype(F32) * col).astype(BF)
    rows = NC * NQ * 16
    pos = iota((rows, FD), 0)
    k, x, unit, core = pos & 3, (pos >> 2) & 3, (pos >> 4) & (NQ - 1), pos >> 9
    source = (x * NC + core) * CW + (unit >> 1) * PAIR + (unit & 1) * 4 + k
    select = ones((iota((rows, FD), 1) == source) & (k < 4 - (unit & 1)))
    for n in range(0, VD, 256):
        out[:, n : n + 256] = dot(select, scaled[:, n : n + 256]).astype(BF)


def head_kernel(columns, head, main, squares, out):
    x = columns[...]
    xf = x.astype(F32)
    d_sq = jnp.sum(xf * xf, axis=0, keepdims=True)
    tail = []
    for v in (*split(d_sq), *split(squares[0:1, :])):
        tail += [v[:, k * L : (k + 1) * L] for k in range(ROWS // L)]
    tail = place(tail, (16, L)).astype(BF)
    n_main = RB * TILES
    for k in range(NZ):
        out[k, 0:n_main, :] = main[k]
        out[k, 2 * n_main :, :] = tail
    xt = xf.T.astype(BF)
    for n in range(0, VD, 256):
        acc = dot(xt, head[:, n : n + 256]).astype(BF)
        for m in range(2):
            t = n_main + (n // L + m) * RB
            for k in range(NZ):
                out[k, t : t + RB, :] = acc[k * RB : (k + 1) * RB, m * L : (m + 1) * L]


def stats_kernel(parts, main_out, draft_out, stats):
    z = lax.axis_index("dp")
    n_main = RB * TILES
    tail = parts[0, 2 * n_main :, :].astype(F32)
    for k in range(1, NZ):
        tail = tail + parts[k, 2 * n_main :, :].astype(F32)
    row, lane = iota((RB, L), 0), iota((RB, L), 1)
    inverse = []
    for n in range(2):
        acc = jnp.zeros((RB, 1), F32)
        for k in range(ROWS // L):
            v = tail[6 * n + k : 6 * n + k + 1] + tail[6 * n + 3 + k : 6 * n + 4 + k]
            acc = acc + jnp.sum(jnp.where(lane + k * L == row + z * RB, v, 0.0), axis=1, keepdims=True)
        inverse.append(lax.rsqrt(acc / D + EPS))
    inv_d, inv_h = inverse
    values = []
    for start, inv, ref in ((0, inv_h, main_out), (n_main, inv_d, draft_out)):
        for t in range(TILES):
            s = start + t * RB
            acc = parts[0, s : s + RB, :].astype(F32)
            for k in range(1, NZ):
                acc = acc + parts[k, s : s + RB, :].astype(F32)
            ref[:, t * L : (t + 1) * L] = acc * inv
        logits = ref[...]
        top = jnp.max(logits, axis=1, keepdims=True)
        total = jnp.sum(jnp.exp(logits - top), axis=1, keepdims=True)
        for v in (top, total):
            values.append(jnp.sum(jnp.where(row == lane, v, 0.0), axis=0, keepdims=True))
    stats[...] = jnp.broadcast_to(place(values, (8, L))[None], stats.shape)


def final_kernel(stats, main, draft, main_out, draft_out):
    diagonal = iota((RB, L), 0) == iota((RB, L), 1)
    every = stats[...]
    for n, (logits, out) in enumerate(((main, main_out), (draft, draft_out))):
        tops, sums = every[:, 2 * n, :], every[:, 2 * n + 1, :]
        top = jnp.max(tops, axis=0, keepdims=True)
        total = jnp.sum(sums * jnp.exp(tops - top), axis=0, keepdims=True)
        top_col = jnp.sum(jnp.where(diagonal, top, 0.0), axis=1, keepdims=True)
        log_col = jnp.log(jnp.sum(jnp.where(diagonal, total, 0.0), axis=1, keepdims=True))
        out[...] = (logits[...] - top_col - log_col).astype(BF)


def exchange(x, groups):
    return lax.all_to_all(x, "vocab", 0, 0, axis_index_groups=groups)


def per_device(
    hidden,
    tokens,
    final_gain,
    hidden_gain,
    embed_gain,
    embed_table,
    proj_hidden,
    proj_embed,
    draft_gain,
    head_weight,
):
    picked = call(pick_kernel, struct((NC * NQ * 8, FD), BF), tokens[None], embed_table)
    share = call(share_kernel, struct((NQ * 8, FD), BF), proj_hidden.T, proj_embed.T)
    half = exchange(picked.reshape(NC, NQ, 8, FD), CORE)
    sent = call(send_kernel, struct((NQ, 16, FD), BF), half, share.reshape(NQ, 8, FD))
    gain = jnp.pad(draft_gain, (0, L - CW))[None]
    unit, weights = call(
        unit_kernel, (struct((NQ, 8, FD), BF), struct((NQ, 8, FD), BF)), exchange(sent, XY), gain
    )
    rows = lax.all_gather(exchange(unit, XY), "vocab", axis_index_groups=CORE).reshape(NC * NQ * 8, FD)

    main, squares = call(
        main_kernel,
        (struct((NZ, RB * TILES, L), BF), struct((8, ROWS), F32)),
        hidden,
        final_gain[None],
        head_weight,
    )
    partial = call(
        proj_kernel,
        struct((NZ, ZR, ROWS), BF),
        rows,
        hidden,
        hidden_gain[None],
        embed_gain[None],
        weights.reshape(NQ * 8, FD),
        squares,
    )
    gained = call(
        gained_kernel,
        struct((NC * NQ * 16, VD), BF),
        rows,
        head_weight,
        scratch=[pltpu.VMEM((FD, VD), BF)],
    )
    joined = call(join_kernel, struct((NQ, 16, ROWS), BF), lax.all_to_all(partial, "dp", 0, 0))
    columns = lax.all_gather(exchange(joined, XY), "vocab", axis_index_groups=CORE)
    blocks = call(
        head_kernel,
        struct((NZ, HR, L), BF),
        columns.reshape(NC * NQ * 16, ROWS),
        gained,
        main,
        squares,
    )
    main_logits, draft_logits, stats = call(
        stats_kernel,
        (struct((RB, VD), F32), struct((RB, VD), F32), struct((NQ * NC, 8, L), F32)),
        lax.all_to_all(blocks, "dp", 0, 0),
    )
    stats = lax.all_to_all(stats, "vocab", 0, 0)
    main_logp, draft_logp = call(
        final_kernel, (struct((RB, VD), BF), struct((RB, VD), BF)), stats, main_logits, draft_logits
    )
    return (main_logp, draft_logp)


def solution(mesh):
    return jax.shard_map(
        per_device,
        mesh=mesh,
        in_specs=(
            P(None, "dp"),
            P(),
            P("dp"),
            P("dp"),
            P("dp"),
            P("vocab", "dp"),
            P("dp", "vocab"),
            P("dp", "vocab"),
            P("vocab"),
            P("dp", "vocab"),
        ),
        out_specs=(P("dp", "vocab"), P("dp", "vocab")),
        check_vma=False,
    )
```

```python
import jax
import jax.numpy as jnp
from jax import lax
from jax.experimental import pallas as pl
from jax.experimental.pallas import tpu as pltpu
from jax.sharding import PartitionSpec as P

EPS = 1e-06
BF, F32 = jnp.bfloat16, jnp.float32
ROWS, D, V = 384, 7168, 65536
NZ, NY, NX, NC = 8, 8, 4, 2
NQ = NY * NX
FD = D // NZ
VD = V // (NQ * NC)
CW = D // (NQ * NC)
RB = ROWS // NZ
UR = RB // (NX * NC)
XR = NC * UR
L = 128
FT = FD // L
ZROWS = 2 * RB + 16
HROWS = RB * (VD // L) + 8
PARAMS = pltpu.CompilerParams(vmem_limit_bytes=48 * 1024 * 1024)


def vid(y, x, c):
    return (y * NX + x) * NC + c


CORE = [[vid(y, x, c) for c in range(NC)] for y in range(NY) for x in range(NX)]
YS = [[vid(y, x, c) for y in range(NY)] for x in range(NX) for c in range(NC)]
XY = [[vid(y, x, c) for y in range(NY) for x in range(NX)] for c in range(NC)]
XC = [[vid(y, x, c) for x in range(NX) for c in range(NC)] for y in range(NY)]


def iota(shape, dim):
    return lax.broadcasted_iota(jnp.int32, shape, dim)


def split(x):
    hi = x.astype(BF).astype(F32)
    return hi, x - hi


def ones(mask):
    return mask.astype(F32).astype(BF)


def dot(a, b):
    return jnp.dot(a, b, preferred_element_type=F32)


def dot_nt(a, b):
    return lax.dot_general(a, b, (((1,), (1,)), ((), ())), preferred_element_type=F32)


def place(rows, shape):
    row = iota(shape, 0)
    out = jnp.zeros(shape, F32)
    for k, v in enumerate(rows):
        out = jnp.where(row == k, v, out)
    return out


def call(kernel, outs, *args, scratch=()):
    single = not isinstance(outs, (list, tuple))
    shapes = [outs] if single else list(outs)
    specs = [pl.BlockSpec(memory_space=pltpu.VMEM) for _ in shapes]
    return pl.pallas_call(
        kernel,
        out_shape=shapes[0] if single else shapes,
        in_specs=[pl.BlockSpec(memory_space=pltpu.VMEM)] * len(args),
        out_specs=specs[0] if single else specs,
        scratch_shapes=list(scratch),
        compiler_params=PARAMS,
    )(*args)


def struct(shape, dtype):
    return jax.ShapeDtypeStruct(shape, dtype)


def pick_kernel(tokens, table, out):
    base = lax.axis_index("vocab") * VD
    rows = NC * NQ * 8
    tok = tokens[...]
    part = iota((8, ROWS), 0)
    high = jnp.broadcast_to(tok >> 8, (8, ROWS)).astype(F32)
    low = jnp.broadcast_to(tok & 255, (8, ROWS)).astype(F32)
    codes = jnp.where(part == 0, high, jnp.where(part == 1, low, 0.0)).astype(BF)
    pos = iota((rows, ROWS), 0)
    step, unit, core = pos & 7, (pos >> 3) & (NQ - 1), pos >> 8
    source = (unit * NC + core) * UR + step
    found = dot_nt(ones((iota((rows, ROWS), 1) == source) & (step < UR)), codes)
    local = (found[:, 0:1] * 256.0 + found[:, 1:2]).astype(jnp.int32) - base
    local = jnp.where((iota((rows, 1), 0) & 7) < UR, local, -1)
    for start in range(0, rows, L):
        hot = ones(iota((L, VD), 1) == local[start : start + L])
        out[start : start + L, :] = dot(hot, table[...]).astype(BF)


def hidden_kernel(hidden, gain, ph, draft_gain, out):
    pos = iota((ROWS, ROWS), 0)
    source = (pos % NQ) * XR + pos // NQ
    select = ones(iota((ROWS, ROWS), 1) == source)
    x = dot(select, (hidden[...].astype(F32) * gain[...]).astype(BF)).astype(BF)
    weights = jnp.concatenate([ph[...], jnp.zeros((L - CW, FD), BF)], axis=0)
    side = dot_nt(x, weights)
    for i in range(XR):
        part = slice(i % FT * L, (i % FT + 1) * L)
        out[i // FT * NQ : (i // FT + 1) * NQ, part] = side[i * NQ : (i + 1) * NQ].astype(BF)
    for i, v in enumerate(split(draft_gain[...])):
        n = XR - FT + i
        out[NQ:, n * L : (n + 1) * L] = jnp.broadcast_to(v.astype(BF), (NQ, L))


def send_kernel(half, side, out):
    row = iota((8, FD), 0)
    lines = side[...].astype(F32)
    for k in range(NQ):
        rows = half[0, k].astype(F32) + half[1, k].astype(F32)
        rows = jnp.where(row == UR, lines[k : k + 1], rows)
        out[k] = jnp.where(row == UR + 1, lines[NQ + k : NQ + k + 1], rows).astype(BF)


def unit_kernel(got, out):
    row = iota((8, FD), 0)
    total = jnp.zeros((8, FD), F32)
    first = [jnp.zeros((8, FD), F32) for _ in range(NX)]
    second = [jnp.zeros((8, FD), F32) for _ in range(NX)]
    for y in range(NY):
        for x in range(NX):
            block = got[y * NX + x].astype(F32)
            total = total + block
            first[x] = jnp.where(row == y, block[UR : UR + 1], first[x])
            second[x] = jnp.where(row == y, block[UR + 1 : UR + 2], second[x])
    for x in range(NX):
        block = jnp.concatenate([total, first[x], second[x]], axis=0).astype(BF)
        for c in range(NC):
            out[x * NC + c] = block


def proj_kernel(got, hidden, embed_gain, weights, out, side):
    y = lax.axis_index("vocab") // (NX * NC)
    core = lax.axis_index("vocab") % NC
    units = [got[k].astype(F32) for k in range(NX * NC)]
    picked = jnp.concatenate([u[0:8] for u in units], axis=0).astype(BF)
    for x in range(NX):
        lines = jnp.where(core == 0, units[x * NC], units[x * NC + 1])[8:24]
        for i in range(XR):
            r, t = i // FT * 8, i % FT * L
            at = (x * XR + i) * 8
            side[at : at + 8, :] = lines[r : r + 8, t : t + L]
    n = (XR - FT) * L
    gain_hi, gain_low = lines[8:16, n : n + L], lines[8:16, n + L : n + 2 * L]
    h = hidden[pl.ds(pl.multiple_of(y * RB, 16), RB), :].astype(F32)
    row, col = iota((RB, 64), 0), iota((RB, 64), 1)
    e = dot(ones(col == (row // UR) * 8 + row % UR), picked)
    lane = iota((RB, L), 1)

    def extra(x):
        hi, low = split(jnp.sum(x * x, axis=1, keepdims=True))
        return jnp.where(lane == CW, hi, jnp.where(lane == CW + 1, low, 0.0))

    extra_h, extra_e = extra(h), extra(e)
    eg = (e * embed_gain[...]).astype(BF)
    pad = jnp.zeros((L - CW, FD), BF)
    for t in range(NY):
        w = jnp.concatenate([weights[t], pad], axis=0)
        out[t, 0:RB, :] = (jnp.where(lane < CW, side[pl.ds(t, RB, stride=8), :], 0.0) + extra_h).astype(BF)
        out[t, RB : 2 * RB, :] = (dot_nt(eg, w) + extra_e).astype(BF)
        out[t, 2 * RB :, :] = place([gain_hi[t : t + 1], gain_low[t : t + 1]], (16, L)).astype(BF)


def join_kernel(parts, out):
    total = parts[0].astype(F32)
    gain = jnp.sum(total[2 * RB :, :], axis=0, keepdims=True)
    for k in range(1, NZ):
        total = total + parts[k].astype(F32)
    lane = iota((RB, L), 1)
    sides = (lane == CW) | (lane == CW + 1)

    def scale(x):
        return lax.rsqrt(jnp.sum(jnp.where(sides, x, 0.0), axis=1, keepdims=True) / D + EPS)

    h, e = total[0:RB], total[RB : 2 * RB]
    inv_h = scale(h)
    projected = jnp.where(lane < CW, h * inv_h + e * scale(e), 0.0)
    sq_hi, sq_low = split(jnp.sum(projected * projected, axis=1, keepdims=True))
    h_hi, h_low = split(inv_h)
    x = projected * gain
    for k, v in enumerate((sq_hi, sq_low, h_hi, h_low)):
        x = jnp.where(lane == CW + k, v, x)
    out[...] = jnp.broadcast_to(x.astype(BF)[None], out.shape)


def head_kernel(rows, head, out, x_ref):
    squares = jnp.zeros((ROWS, L), F32)
    for x in range(NX):
        for c in range(NC):
            a = jnp.concatenate([rows[c, y * NX + x] for y in range(NY)], axis=0)
            j = x * NC + c
            x_ref[:, j * CW : (j + 1) * CW] = a[:, 0:CW]
            squares = squares + a.astype(F32)
            if j == 0:
                scales = a.astype(F32)
    lane = iota((ROWS, L), 1)
    sq = jnp.sum(jnp.where((lane == CW) | (lane == CW + 1), squares, 0.0), axis=1, keepdims=True)
    inv_h = jnp.sum(jnp.where((lane == CW + 2) | (lane == CW + 3), scales, 0.0), axis=1, keepdims=True)
    diagonal = iota((RB, L), 0) == iota((RB, L), 1)
    part = iota((8, L), 0)
    for k in range(NZ):
        tail = jnp.zeros((8, L), F32)
        for n, col in enumerate((sq, inv_h)):
            line = jnp.sum(jnp.where(diagonal, col[k * RB : (k + 1) * RB], 0.0), axis=0, keepdims=True)
            hi, low = split(line)
            tail = jnp.where(part == 2 * n, hi, jnp.where(part == 2 * n + 1, low, tail))
        out[k, HROWS - 8 :, :] = tail.astype(BF)
    for n in range(0, VD, 256):
        acc = jnp.dot(x_ref[...], head[:, n : n + 256], preferred_element_type=F32).astype(BF)
        for m in range(2):
            tile = n // L + m
            for k in range(NZ):
                out[k, tile * RB : (tile + 1) * RB, :] = acc[k * RB : (k + 1) * RB, m * L : (m + 1) * L]


def stats_kernel(parts, main, main_out, draft_out, stats):
    diagonal = iota((RB, L), 0) == iota((RB, L), 1)

    def column(line):
        return jnp.sum(jnp.where(diagonal, line, 0.0), axis=1, keepdims=True)

    def line(col):
        return jnp.sum(jnp.where(diagonal, col, 0.0), axis=0, keepdims=True)

    tail = parts[0, HROWS - 8 :, :].astype(F32)
    inv_h = column(tail[2:3] + tail[3:4])
    for k in range(1, NZ):
        tail = tail + parts[k, HROWS - 8 :, :].astype(F32)
    inv_d = lax.rsqrt(column(tail[0:1] + tail[1:2]) / D + EPS)
    main_logits = main[...] * inv_h
    main_out[...] = main_logits
    for t in range(VD // L):
        acc = parts[0, t * RB : (t + 1) * RB, :].astype(F32)
        for k in range(1, NZ):
            acc = acc + parts[k, t * RB : (t + 1) * RB, :].astype(F32)
        draft_out[:, t * L : (t + 1) * L] = acc * inv_d
    draft_logits = draft_out[...]
    part = iota((8, L), 0)
    value = jnp.zeros((8, L), F32)
    for n, logits in enumerate((main_logits, draft_logits)):
        top = jnp.max(logits, axis=1, keepdims=True)
        total = jnp.sum(jnp.exp(logits - top), axis=1, keepdims=True)
        value = jnp.where(part == 2 * n, line(top), jnp.where(part == 2 * n + 1, line(total), value))
    stats[...] = jnp.broadcast_to(value[None], stats.shape)


def final_kernel(stats, main, draft, main_out, draft_out):
    diagonal = iota((RB, L), 0) == iota((RB, L), 1)
    every = stats[...]
    for n, (logits, out) in enumerate(((main, main_out), (draft, draft_out))):
        tops, sums = every[:, 2 * n, :], every[:, 2 * n + 1, :]
        top = jnp.max(tops, axis=0, keepdims=True)
        total = jnp.sum(sums * jnp.exp(tops - top), axis=0, keepdims=True)
        top_col = jnp.sum(jnp.where(diagonal, top, 0.0), axis=1, keepdims=True)
        log_col = jnp.log(jnp.sum(jnp.where(diagonal, total, 0.0), axis=1, keepdims=True))
        out[...] = (logits[...] - top_col - log_col).astype(BF)


def exchange(x, groups):
    return lax.all_to_all(x, "vocab", 0, 0, axis_index_groups=groups)


def per_device(
    hidden,
    tokens,
    final_gain,
    hidden_gain,
    embed_gain,
    embed_table,
    proj_hidden,
    proj_embed,
    draft_gain,
    head_weight,
):
    weights = lax.all_gather(proj_embed.T, "vocab", axis_index_groups=YS)

    picked = call(pick_kernel, struct((NC * NQ * 8, FD), BF), tokens[None], embed_table)
    half = exchange(picked.reshape(NC, NQ, 8, FD), CORE)
    gain = jnp.pad(draft_gain, (0, L - CW))[None]
    side = call(hidden_kernel, struct((2 * NQ, FD), BF), hidden, hidden_gain[None], proj_hidden.T, gain)
    sent = call(send_kernel, struct((NQ, 8, FD), BF), half, side)
    unit = call(unit_kernel, struct((NX * NC, 24, FD), BF), exchange(sent, XY))
    got = exchange(unit, XC)

    main_in = (hidden.astype(F32) * final_gain).astype(BF)
    main_part = jnp.dot(main_in, head_weight, preferred_element_type=F32)
    main = lax.psum_scatter(main_part, "dp", scatter_dimension=0, tiled=True)

    partial = call(
        proj_kernel,
        struct((NY, ZROWS, L), BF),
        got,
        hidden,
        embed_gain[None],
        weights,
        scratch=[pltpu.VMEM((RB * 8, L), F32)],
    )
    joined = call(join_kernel, struct((NQ, RB, L), BF), lax.all_to_all(partial, "dp", 0, 0))
    rows = lax.all_gather(exchange(joined, XY), "vocab", axis_index_groups=CORE)
    blocks = call(
        head_kernel,
        struct((NZ, HROWS, L), BF),
        rows,
        head_weight,
        scratch=[pltpu.VMEM((ROWS, FD), BF)],
    )
    parts = lax.all_to_all(blocks, "dp", 0, 0)
    main_logits, draft_logits, stats = call(
        stats_kernel,
        (struct((RB, VD), F32), struct((RB, VD), F32), struct((NQ * NC, 8, L), F32)),
        parts,
        main,
    )
    stats = lax.all_to_all(stats, "vocab", 0, 0)
    main_logp, draft_logp = call(
        final_kernel, (struct((RB, VD), BF), struct((RB, VD), BF)), stats, main_logits, draft_logits
    )
    return (main_logp, draft_logp)


def solution(mesh):
    return jax.shard_map(
        per_device,
        mesh=mesh,
        in_specs=(
            P(None, "dp"),
            P(),
            P("dp"),
            P("dp"),
            P("dp"),
            P("vocab", "dp"),
            P("dp", "vocab"),
            P("dp", "vocab"),
            P("vocab"),
            P("dp", "vocab"),
        ),
        out_specs=(P("dp", "vocab"), P("dp", "vocab")),
        check_vma=False,
    )
```

```python
import jax
import jax.numpy as jnp
from jax import lax
from jax.experimental import pallas as pl
from jax.experimental.pallas import tpu as pltpu
from jax.sharding import PartitionSpec as P

EPS = 1e-06
BF, F32 = jnp.bfloat16, jnp.float32
ROWS, D, V = 384, 7168, 65536
NZ, NY, NX, NC = 8, 8, 4, 2
NQ = NY * NX
FD = D // NZ
VD = V // (NQ * NC)
CW = D // (NQ * NC)
RB = ROWS // NZ
UR = RB // (NX * NC)
XR = NC * UR
L = 128
FT = FD // L
ZROWS = 2 * RB + 16
HROWS = RB * (VD // L) + 8


def vid(y, x, c):
    return (y * NX + x) * NC + c


CORE = [[vid(y, x, c) for c in range(NC)] for y in range(NY) for x in range(NX)]
YS = [[vid(y, x, c) for y in range(NY)] for x in range(NX) for c in range(NC)]
XY = [[vid(y, x, c) for y in range(NY) for x in range(NX)] for c in range(NC)]
XC = [[vid(y, x, c) for x in range(NX) for c in range(NC)] for y in range(NY)]


def iota(shape, dim):
    return lax.broadcasted_iota(jnp.int32, shape, dim)


def split(x):
    hi = x.astype(BF).astype(F32)
    return hi, x - hi


def ones(mask):
    return mask.astype(F32).astype(BF)


def dot(a, b):
    return jnp.dot(a, b, preferred_element_type=F32)


def dot_nt(a, b):
    return lax.dot_general(a, b, (((1,), (1,)), ((), ())), preferred_element_type=F32)


def place(rows, shape):
    row = iota(shape, 0)
    out = jnp.zeros(shape, F32)
    for k, v in enumerate(rows):
        out = jnp.where(row == k, v, out)
    return out


def call(kernel, outs, *args, scratch=(), far=(), room=48 * 1024):
    single = not isinstance(outs, (list, tuple))
    shapes = [outs] if single else list(outs)
    specs = [pl.BlockSpec(memory_space=pltpu.VMEM) for _ in shapes]
    return pl.pallas_call(
        kernel,
        out_shape=shapes[0] if single else shapes,
        in_specs=[pl.BlockSpec(memory_space=pltpu.HBM if k in far else pltpu.VMEM) for k in range(len(args))],
        out_specs=specs[0] if single else specs,
        scratch_shapes=list(scratch),
        compiler_params=pltpu.CompilerParams(vmem_limit_bytes=room * 1024),
    )(*args)


def struct(shape, dtype):
    return jax.ShapeDtypeStruct(shape, dtype)


def front_kernel(tokens, gain, draft_gain, hidden, ph, table, out, side, hidden_v, ph_v, table_v, sems):
    copies = [
        pltpu.make_async_copy(src, dst, sems.at[k])
        for k, (src, dst) in enumerate(((hidden, hidden_v), (ph, ph_v), (table, table_v)))
    ]
    for copy in copies:
        copy.start()
    pos = iota((ROWS, ROWS), 0)
    source = (pos % NQ) * XR + pos // NQ
    select = ones(iota((ROWS, ROWS), 1) == source)
    base = lax.axis_index("vocab") * VD
    rows = NC * NQ * 8
    tok = tokens[...]
    part = iota((8, ROWS), 0)
    high = jnp.broadcast_to(tok >> 8, (8, ROWS)).astype(F32)
    low = jnp.broadcast_to(tok & 255, (8, ROWS)).astype(F32)
    codes = jnp.where(part == 0, high, jnp.where(part == 1, low, 0.0)).astype(BF)
    pos = iota((rows, ROWS), 0)
    step, unit, core = pos & 7, (pos >> 3) & (NQ - 1), pos >> 8
    source = (unit * NC + core) * UR + step
    found = dot_nt(ones((iota((rows, ROWS), 1) == source) & (step < UR)), codes)
    local = (found[:, 0:1] * 256.0 + found[:, 1:2]).astype(jnp.int32) - base
    local = jnp.where((iota((rows, 1), 0) & 7) < UR, local, -1)
    copies[0].wait()
    x = dot(select, (hidden_v[...].astype(F32) * gain[...]).astype(BF)).astype(BF)
    copies[1].wait()
    weights = jnp.concatenate([ph_v[...], jnp.zeros((L - CW, FD), BF)], axis=0)
    lines = dot_nt(x, weights)
    for i in range(XR):
        part = slice(i % FT * L, (i % FT + 1) * L)
        side[i // FT * NQ : (i // FT + 1) * NQ, part] = lines[i * NQ : (i + 1) * NQ].astype(BF)
    for i, v in enumerate(split(draft_gain[...])):
        n = XR - FT + i
        side[NQ:, n * L : (n + 1) * L] = jnp.broadcast_to(v.astype(BF), (NQ, L))
    copies[2].wait()
    for start in range(0, rows, L):
        hot = ones(iota((L, VD), 1) == local[start : start + L])
        out[start : start + L, :] = dot(hot, table_v[...]).astype(BF)


def send_kernel(half, side, out):
    row = iota((8, FD), 0)
    lines = side[...].astype(F32)
    for k in range(NQ):
        rows = half[0, k].astype(F32) + half[1, k].astype(F32)
        rows = jnp.where(row == UR, lines[k : k + 1], rows)
        out[k] = jnp.where(row == UR + 1, lines[NQ + k : NQ + k + 1], rows).astype(BF)


def unit_kernel(got, out):
    row = iota((8, FD), 0)
    total = jnp.zeros((8, FD), F32)
    first = [jnp.zeros((8, FD), F32) for _ in range(NX)]
    second = [jnp.zeros((8, FD), F32) for _ in range(NX)]
    for y in range(NY):
        for x in range(NX):
            block = got[y * NX + x].astype(F32)
            total = total + block
            first[x] = jnp.where(row == y, block[UR : UR + 1], first[x])
            second[x] = jnp.where(row == y, block[UR + 1 : UR + 2], second[x])
    for x in range(NX):
        block = jnp.concatenate([total, first[x], second[x]], axis=0).astype(BF)
        for c in range(NC):
            out[x * NC + c] = block


def proj_kernel(got, hidden, embed_gain, weights, out, side, hidden_v, weights_v, sems):
    y = lax.axis_index("vocab") // (NX * NC)
    mine = hidden.at[pl.ds(pl.multiple_of(y * RB, 16), RB), :]
    copies = [
        pltpu.make_async_copy(mine, hidden_v, sems.at[0]),
        pltpu.make_async_copy(weights, weights_v, sems.at[1]),
    ]
    for copy in copies:
        copy.start()
    core = lax.axis_index("vocab") % NC
    units = [got[k].astype(F32) for k in range(NX * NC)]
    picked = jnp.concatenate([u[0:8] for u in units], axis=0).astype(BF)
    for x in range(NX):
        lines = jnp.where(core == 0, units[x * NC], units[x * NC + 1])[8:24]
        for i in range(XR):
            r, t = i // FT * 8, i % FT * L
            at = (x * XR + i) * 8
            side[at : at + 8, :] = lines[r : r + 8, t : t + L]
    n = (XR - FT) * L
    gain_hi, gain_low = lines[8:16, n : n + L], lines[8:16, n + L : n + 2 * L]
    copies[0].wait()
    h = hidden_v[...].astype(F32)
    row, col = iota((RB, 64), 0), iota((RB, 64), 1)
    e = dot(ones(col == (row // UR) * 8 + row % UR), picked)
    lane = iota((RB, L), 1)

    def extra(x):
        hi, low = split(jnp.sum(x * x, axis=1, keepdims=True))
        return jnp.where(lane == CW, hi, jnp.where(lane == CW + 1, low, 0.0))

    extra_h, extra_e = extra(h), extra(e)
    eg = (e * embed_gain[...]).astype(BF)
    pad = jnp.zeros((L - CW, FD), BF)
    copies[1].wait()
    for t in range(NY):
        w = jnp.concatenate([weights_v[t], pad], axis=0)
        out[t, 0:RB, :] = (jnp.where(lane < CW, side[pl.ds(t, RB, stride=8), :], 0.0) + extra_h).astype(BF)
        out[t, RB : 2 * RB, :] = (dot_nt(eg, w) + extra_e).astype(BF)
        out[t, 2 * RB :, :] = place([gain_hi[t : t + 1], gain_low[t : t + 1]], (16, L)).astype(BF)


def join_kernel(parts, out):
    total = parts[0].astype(F32)
    gain = jnp.sum(total[2 * RB :, :], axis=0, keepdims=True)
    for k in range(1, NZ):
        total = total + parts[k].astype(F32)
    lane = iota((RB, L), 1)
    sides = (lane == CW) | (lane == CW + 1)

    def scale(x):
        return lax.rsqrt(jnp.sum(jnp.where(sides, x, 0.0), axis=1, keepdims=True) / D + EPS)

    h, e = total[0:RB], total[RB : 2 * RB]
    inv_h = scale(h)
    projected = jnp.where(lane < CW, h * inv_h + e * scale(e), 0.0)
    sq_hi, sq_low = split(jnp.sum(projected * projected, axis=1, keepdims=True))
    h_hi, h_low = split(inv_h)
    x = projected * gain
    for k, v in enumerate((sq_hi, sq_low, h_hi, h_low)):
        x = jnp.where(lane == CW + k, v, x)
    out[...] = jnp.broadcast_to(x.astype(BF)[None], out.shape)


def head_kernel(rows, head, out, x_ref):
    squares = jnp.zeros((ROWS, L), F32)
    for x in range(NX):
        for c in range(NC):
            a = jnp.concatenate([rows[c, y * NX + x] for y in range(NY)], axis=0)
            j = x * NC + c
            x_ref[:, j * CW : (j + 1) * CW] = a[:, 0:CW]
            squares = squares + a.astype(F32)
    lane = iota((ROWS, L), 1)
    sq = jnp.sum(jnp.where((lane == CW) | (lane == CW + 1), squares, 0.0), axis=1, keepdims=True)
    diagonal = iota((RB, L), 0) == iota((RB, L), 1)
    part = iota((8, L), 0)
    for k in range(NZ):
        line = jnp.sum(jnp.where(diagonal, sq[k * RB : (k + 1) * RB], 0.0), axis=0, keepdims=True)
        out[k, HROWS - 8 :, :] = place(split(line), (8, L)).astype(BF)
    for n in range(0, VD, 256):
        acc = jnp.dot(x_ref[...], head[:, n : n + 256], preferred_element_type=F32).astype(BF)
        for m in range(2):
            tile = n // L + m
            for k in range(NZ):
                out[k, tile * RB : (tile + 1) * RB, :] = acc[k * RB : (k + 1) * RB, m * L : (m + 1) * L]


def summary(logits):
    diagonal = iota((RB, L), 0) == iota((RB, L), 1)
    top = jnp.max(logits, axis=1, keepdims=True)
    total = jnp.sum(jnp.exp(logits - top), axis=1, keepdims=True)
    return [jnp.sum(jnp.where(diagonal, v, 0.0), axis=0, keepdims=True) for v in (top, total)]


def main_kernel(rows, sums, out, stats):
    z = lax.axis_index("dp")
    lane = iota((RB, L), 1)
    block = rows[0, z * NX].astype(F32)
    scale = jnp.sum(jnp.where((lane == CW + 2) | (lane == CW + 3), block, 0.0), axis=1, keepdims=True)
    logits = sums[...] * scale
    out[...] = logits
    stats[...] = place(summary(logits), (8, L))


def stats_kernel(parts, main_stats, out, stats):
    diagonal = iota((RB, L), 0) == iota((RB, L), 1)
    tail = parts[0, HROWS - 8 :, :].astype(F32)
    for k in range(1, NZ):
        tail = tail + parts[k, HROWS - 8 :, :].astype(F32)
    squares = jnp.sum(jnp.where(diagonal, tail[0:1] + tail[1:2], 0.0), axis=1, keepdims=True)
    scale = lax.rsqrt(squares / D + EPS)
    for t in range(VD // L):
        acc = parts[0, t * RB : (t + 1) * RB, :].astype(F32)
        for k in range(1, NZ):
            acc = acc + parts[k, t * RB : (t + 1) * RB, :].astype(F32)
        out[:, t * L : (t + 1) * L] = acc * scale
    both = place([main_stats[0:1, :], main_stats[1:2, :], *summary(out[...])], (8, L))
    stats[...] = jnp.broadcast_to(both[None], stats.shape)


def final_kernel(stats, main, draft, main_out, draft_out):
    top = stats[0]
    for k in range(1, NQ * NC):
        top = jnp.maximum(top, stats[k])
    total = jnp.zeros((8, L), F32)
    for k in range(NQ * NC):
        total = total + stats[k] * pltpu.roll(jnp.exp(stats[k] - top), 1, 0)
    diagonal = iota((RB, L), 0) == iota((RB, L), 1)

    def column(line):
        return jnp.sum(jnp.where(diagonal, line, 0.0), axis=1, keepdims=True)

    for n, (logits, out) in enumerate(((main, main_out), (draft, draft_out))):
        shift = column(top[2 * n : 2 * n + 1])
        log_total = jnp.log(column(total[2 * n + 1 : 2 * n + 2]))
        out[...] = (logits[...] - shift - log_total).astype(BF)


def exchange(x, groups):
    return lax.all_to_all(x, "vocab", 0, 0, axis_index_groups=groups)


def per_device(
    hidden,
    tokens,
    final_gain,
    hidden_gain,
    embed_gain,
    embed_table,
    proj_hidden,
    proj_embed,
    draft_gain,
    head_weight,
):
    weights = lax.all_gather(proj_embed.T, "vocab", axis_index_groups=YS)

    gain = jnp.pad(draft_gain, (0, L - CW))[None]
    picked, side = call(
        front_kernel,
        (struct((NC * NQ * 8, FD), BF), struct((2 * NQ, FD), BF)),
        tokens[None],
        hidden_gain[None],
        gain,
        hidden,
        proj_hidden.T,
        embed_table,
        far=(3, 4, 5),
        room=63 * 1024,
        scratch=[
            pltpu.VMEM((ROWS, FD), BF),
            pltpu.VMEM((CW, FD), BF),
            pltpu.VMEM((VD, FD), BF),
            pltpu.SemaphoreType.DMA((3,)),
        ],
    )
    half = exchange(picked.reshape(NC, NQ, 8, FD), CORE)
    sent = call(send_kernel, struct((NQ, 8, FD), BF), half, side)
    unit = call(unit_kernel, struct((NX * NC, 24, FD), BF), exchange(sent, XY))
    got = exchange(unit, XC)

    main_in = (hidden.astype(F32) * final_gain).astype(BF)
    main_part = jnp.dot(main_in, head_weight, preferred_element_type=F32)
    main = lax.psum_scatter(main_part, "dp", scatter_dimension=0, tiled=True)

    partial = call(
        proj_kernel,
        struct((NY, ZROWS, L), BF),
        got,
        hidden,
        embed_gain[None],
        weights,
        far=(1, 3),
        room=64000,
        scratch=[
            pltpu.VMEM((RB * 8, L), F32),
            pltpu.VMEM((RB, FD), BF),
            pltpu.VMEM((NY, CW, FD), BF),
            pltpu.SemaphoreType.DMA((2,)),
        ],
    )
    joined = call(join_kernel, struct((NQ, RB, L), BF), lax.all_to_all(partial, "dp", 0, 0))
    rows = lax.all_gather(exchange(joined, XY), "vocab", axis_index_groups=CORE)
    blocks = call(
        head_kernel,
        struct((NZ, HROWS, L), BF),
        rows,
        head_weight,
        scratch=[pltpu.VMEM((ROWS, FD), BF)],
    )
    parts = lax.all_to_all(blocks, "dp", 0, 0)
    main_logits, main_stats = call(main_kernel, (struct((RB, VD), F32), struct((8, L), F32)), rows, main)
    draft_logits, stats = call(
        stats_kernel, (struct((RB, VD), F32), struct((NQ * NC, 8, L), F32)), parts, main_stats
    )
    stats = lax.all_to_all(stats, "vocab", 0, 0)
    main_logp, draft_logp = call(
        final_kernel, (struct((RB, VD), BF), struct((RB, VD), BF)), stats, main_logits, draft_logits
    )
    return (main_logp, draft_logp)


def solution(mesh):
    return jax.shard_map(
        per_device,
        mesh=mesh,
        in_specs=(
            P(None, "dp"),
            P(),
            P("dp"),
            P("dp"),
            P("dp"),
            P("vocab", "dp"),
            P("dp", "vocab"),
            P("dp", "vocab"),
            P("vocab"),
            P("dp", "vocab"),
        ),
        out_specs=(P("dp", "vocab"), P("dp", "vocab")),
        check_vma=False,
    )
```

```python
import jax
import jax.numpy as jnp
from jax import lax
from jax.experimental import pallas as pl
from jax.experimental.pallas import tpu as pltpu
from jax.sharding import PartitionSpec as P

EPS = 1e-06
BF, F32 = jnp.bfloat16, jnp.float32
ROWS, D, V = 384, 7168, 65536
NZ, NY, NX, NC = 8, 8, 4, 2
NQ = NY * NX
FD = D // NZ
VD = V // (NQ * NC)
CW = D // (NQ * NC)
RB = ROWS // NZ
UR = RB // (NX * NC)
XR = NC * UR
L = 128
FT = FD // L
ZROWS = 2 * RB + 16
HROWS = RB * (VD // L) + 8
PARAMS = pltpu.CompilerParams(vmem_limit_bytes=48 * 1024 * 1024)


def vid(y, x, c):
    return (y * NX + x) * NC + c


CORE = [[vid(y, x, c) for c in range(NC)] for y in range(NY) for x in range(NX)]
YS = [[vid(y, x, c) for y in range(NY)] for x in range(NX) for c in range(NC)]
XY = [[vid(y, x, c) for y in range(NY) for x in range(NX)] for c in range(NC)]
XS = [[vid(y, x, c) for x in range(NX)] for y in range(NY) for c in range(NC)]


def iota(shape, dim):
    return lax.broadcasted_iota(jnp.int32, shape, dim)


def split(x):
    hi = x.astype(BF).astype(F32)
    return hi, x - hi


def ones(mask):
    return mask.astype(F32).astype(BF)


def dot(a, b):
    return jnp.dot(a, b, preferred_element_type=F32)


def dot_nt(a, b):
    return lax.dot_general(a, b, (((1,), (1,)), ((), ())), preferred_element_type=F32)


def place(rows, shape):
    row = iota(shape, 0)
    out = jnp.zeros(shape, F32)
    for k, v in enumerate(rows):
        out = jnp.where(row == k, v, out)
    return out


def call(kernel, outs, *args, scratch=(), space=pltpu.VMEM):
    single = not isinstance(outs, (list, tuple))
    shapes = [outs] if single else list(outs)
    specs = [pl.BlockSpec(memory_space=space) for _ in shapes]
    return pl.pallas_call(
        kernel,
        out_shape=shapes[0] if single else shapes,
        in_specs=[pl.BlockSpec(memory_space=pltpu.VMEM)] * len(args),
        out_specs=specs[0] if single else specs,
        scratch_shapes=list(scratch),
        compiler_params=PARAMS,
    )(*args)


def struct(shape, dtype):
    return jax.ShapeDtypeStruct(shape, dtype)


def pick_kernel(tokens, table, out, buf, sems):
    base = lax.axis_index("vocab") * VD
    rows = NC * NQ * 8
    tok = tokens[...].reshape(1, ROWS)
    part = iota((8, ROWS), 0)
    high = jnp.broadcast_to(tok >> 8, (8, ROWS)).astype(F32)
    low = jnp.broadcast_to(tok & 255, (8, ROWS)).astype(F32)
    codes = jnp.where(part == 0, high, jnp.where(part == 1, low, 0.0)).astype(BF)
    pos = iota((rows, ROWS), 0)
    step, unit, core = pos & 7, (pos >> 3) & (NQ - 1), pos >> 8
    source = (unit * NC + core) * UR + step
    found = dot_nt(ones((iota((rows, ROWS), 1) == source) & (step < UR)), codes)
    local = (found[:, 0:1] * 256.0 + found[:, 1:2]).astype(jnp.int32) - base
    local = jnp.where((iota((rows, 1), 0) & 7) < UR, local, -1)
    copies = []
    for start in range(0, rows, L):
        hot = ones(iota((L, VD), 1) == local[start : start + L])
        buf[start : start + L, :] = dot(hot, table[...]).astype(BF)
        part = pl.ds(start, L)
        copies.append(pltpu.make_async_copy(buf.at[part], out.at[part], sems.at[start // L]))
        copies[-1].start()
    for copy in copies:
        copy.wait()


def hidden_kernel(hidden, gain, ph, draft_gain, out):
    pos = iota((ROWS, ROWS), 0)
    source = (pos % NQ) * XR + pos // NQ
    select = ones(iota((ROWS, ROWS), 1) == source)
    x = dot(select, (hidden[...].astype(F32) * gain[...]).astype(BF)).astype(BF)
    weights = jnp.concatenate([ph[...], jnp.zeros((L - CW, FD), BF)], axis=0)
    side = dot_nt(x, weights)
    for i in range(XR):
        part = slice(i % FT * L, (i % FT + 1) * L)
        out[i // FT * NQ : (i // FT + 1) * NQ, part] = side[i * NQ : (i + 1) * NQ].astype(BF)
    for i, v in enumerate(split(draft_gain[...])):
        n = XR - FT + i
        out[NQ:, n * L : (n + 1) * L] = jnp.broadcast_to(v.astype(BF), (NQ, L))


def send_kernel(half, side, out, buf, sems):
    row = iota((8, FD), 0)
    lines = side[...].astype(F32)
    copies = []
    for k in range(NQ):
        rows = half[0, k].astype(F32) + half[1, k].astype(F32)
        rows = jnp.where(row == UR, lines[k : k + 1], rows)
        buf[k] = jnp.where(row == UR + 1, lines[NQ + k : NQ + k + 1], rows).astype(BF)
        if k % 8 == 7:
            part = pl.ds(k - 7, 8)
            copies.append(pltpu.make_async_copy(buf.at[part], out.at[part], sems.at[k // 8]))
            copies[-1].start()
    for copy in copies:
        copy.wait()


def unit_kernel(got, out):
    row = iota((8, FD), 0)
    total = jnp.zeros((8, FD), F32)
    first = [jnp.zeros((8, FD), F32) for _ in range(NX)]
    second = [jnp.zeros((8, FD), F32) for _ in range(NX)]
    for y in range(NY):
        for x in range(NX):
            block = got[y * NX + x].astype(F32)
            total = total + block
            first[x] = jnp.where(row == y, block[UR : UR + 1], first[x])
            second[x] = jnp.where(row == y, block[UR + 1 : UR + 2], second[x])
    for x in range(NX):
        out[x] = jnp.concatenate([total, first[x], second[x]], axis=0).astype(BF)


def proj_kernel(got, hidden, embed_gain, weights, out, side):
    y = lax.axis_index("vocab") // (NX * NC)
    core = lax.axis_index("vocab") % NC
    units = [got[c, x].astype(F32) for x in range(NX) for c in range(NC)]
    picked = jnp.concatenate([u[0:8] for u in units], axis=0).astype(BF)
    for x in range(NX):
        lines = jnp.where(core == 0, units[x * NC], units[x * NC + 1])[8:24]
        for i in range(XR):
            r, t = i // FT * 8, i % FT * L
            at = (x * XR + i) * 8
            side[at : at + 8, :] = lines[r : r + 8, t : t + L]
    n = (XR - FT) * L
    gain_hi, gain_low = lines[8:16, n : n + L], lines[8:16, n + L : n + 2 * L]
    h = hidden[pl.ds(pl.multiple_of(y * RB, 16), RB), :].astype(F32)
    row, col = iota((RB, 64), 0), iota((RB, 64), 1)
    e = dot(ones(col == (row // UR) * 8 + row % UR), picked)
    lane = iota((RB, L), 1)

    def extra(x):
        hi, low = split(jnp.sum(x * x, axis=1, keepdims=True))
        return jnp.where(lane == CW, hi, jnp.where(lane == CW + 1, low, 0.0))

    extra_h, extra_e = extra(h), extra(e)
    eg = (e * embed_gain[...]).astype(BF)
    pad = jnp.zeros((L - CW, FD), BF)
    for t in range(NY):
        w = jnp.concatenate([weights[t], pad], axis=0)
        out[t, 0:RB, :] = (jnp.where(lane < CW, side[pl.ds(t, RB, stride=8), :], 0.0) + extra_h).astype(BF)
        out[t, RB : 2 * RB, :] = (dot_nt(eg, w) + extra_e).astype(BF)
        out[t, 2 * RB :, :] = place([gain_hi[t : t + 1], gain_low[t : t + 1]], (16, L)).astype(BF)


def join_kernel(parts, out):
    total = parts[0].astype(F32)
    gain = jnp.sum(total[2 * RB :, :], axis=0, keepdims=True)
    for k in range(1, NZ):
        total = total + parts[k].astype(F32)
    lane = iota((RB, L), 1)
    sides = (lane == CW) | (lane == CW + 1)

    def scale(x):
        return lax.rsqrt(jnp.sum(jnp.where(sides, x, 0.0), axis=1, keepdims=True) / D + EPS)

    h, e = total[0:RB], total[RB : 2 * RB]
    inv_h = scale(h)
    projected = jnp.where(lane < CW, h * inv_h + e * scale(e), 0.0)
    sq_hi, sq_low = split(jnp.sum(projected * projected, axis=1, keepdims=True))
    h_hi, h_low = split(inv_h)
    x = projected * gain
    for k, v in enumerate((sq_hi, sq_low, h_hi, h_low)):
        x = jnp.where(lane == CW + k, v, x)
    out[...] = jnp.broadcast_to(x.astype(BF)[None], out.shape)


def head_kernel(rows, head, out, x_ref):
    squares = jnp.zeros((ROWS, L), F32)
    for x in range(NX):
        for c in range(NC):
            a = jnp.concatenate([rows[c, y * NX + x] for y in range(NY)], axis=0)
            j = x * NC + c
            x_ref[:, j * CW : (j + 1) * CW] = a[:, 0:CW]
            squares = squares + a.astype(F32)
    lane = iota((ROWS, L), 1)
    sq = jnp.sum(jnp.where((lane == CW) | (lane == CW + 1), squares, 0.0), axis=1, keepdims=True)
    diagonal = iota((RB, L), 0) == iota((RB, L), 1)
    part = iota((8, L), 0)
    for k in range(NZ):
        line = jnp.sum(jnp.where(diagonal, sq[k * RB : (k + 1) * RB], 0.0), axis=0, keepdims=True)
        out[k, HROWS - 8 :, :] = place(split(line), (8, L)).astype(BF)
    for n in range(0, VD, 256):
        acc = jnp.dot(x_ref[...], head[:, n : n + 256], preferred_element_type=F32).astype(BF)
        for m in range(2):
            tile = n // L + m
            for k in range(NZ):
                out[k, tile * RB : (tile + 1) * RB, :] = acc[k * RB : (k + 1) * RB, m * L : (m + 1) * L]


def summary(logits):
    diagonal = iota((RB, L), 0) == iota((RB, L), 1)
    top = jnp.max(logits, axis=1, keepdims=True)
    total = jnp.sum(jnp.exp(logits - top), axis=1, keepdims=True)
    return [jnp.sum(jnp.where(diagonal, v, 0.0), axis=0, keepdims=True) for v in (top, total)]


def main_kernel(rows, sums, out, stats):
    z = lax.axis_index("dp")
    lane = iota((RB, L), 1)
    block = rows[0, z * NX].astype(F32)
    scale = jnp.sum(jnp.where((lane == CW + 2) | (lane == CW + 3), block, 0.0), axis=1, keepdims=True)
    logits = sums[...] * scale
    out[...] = logits
    stats[...] = place(summary(logits), (8, L))


def stats_kernel(parts, main_stats, out, stats):
    diagonal = iota((RB, L), 0) == iota((RB, L), 1)
    tail = parts[0, HROWS - 8 :, :].astype(F32)
    for k in range(1, NZ):
        tail = tail + parts[k, HROWS - 8 :, :].astype(F32)
    squares = jnp.sum(jnp.where(diagonal, tail[0:1] + tail[1:2], 0.0), axis=1, keepdims=True)
    scale = lax.rsqrt(squares / D + EPS)
    for t in range(VD // L):
        acc = parts[0, t * RB : (t + 1) * RB, :].astype(F32)
        for k in range(1, NZ):
            acc = acc + parts[k, t * RB : (t + 1) * RB, :].astype(F32)
        out[:, t * L : (t + 1) * L] = acc * scale
    both = place([main_stats[0:1, :], main_stats[1:2, :], *summary(out[...])], (8, L))
    stats[...] = jnp.broadcast_to(both[None], stats.shape)


def final_kernel(stats, main, draft, main_out, draft_out):
    top = stats[0]
    for k in range(1, NQ * NC):
        top = jnp.maximum(top, stats[k])
    total = jnp.zeros((8, L), F32)
    for k in range(NQ * NC):
        total = total + stats[k] * pltpu.roll(jnp.exp(stats[k] - top), 1, 0)
    diagonal = iota((RB, L), 0) == iota((RB, L), 1)

    def column(line):
        return jnp.sum(jnp.where(diagonal, line, 0.0), axis=1, keepdims=True)

    for n, (logits, out) in enumerate(((main, main_out), (draft, draft_out))):
        shift = column(top[2 * n : 2 * n + 1])
        log_total = jnp.log(column(total[2 * n + 1 : 2 * n + 2]))
        out[...] = (logits[...] - shift - log_total).astype(BF)


def exchange(x, groups):
    return lax.all_to_all(x, "vocab", 0, 0, axis_index_groups=groups)


def per_device(
    hidden,
    tokens,
    final_gain,
    hidden_gain,
    embed_gain,
    embed_table,
    proj_hidden,
    proj_embed,
    draft_gain,
    head_weight,
):
    weights = lax.all_gather(proj_embed.T, "vocab", axis_index_groups=YS)

    picked = call(
        pick_kernel,
        struct((NC * NQ * 8, FD), BF),
        tokens,
        embed_table,
        scratch=[pltpu.VMEM((NC * NQ * 8, FD), BF), pltpu.SemaphoreType.DMA((NC * NQ * 8 // L,))],
        space=pltpu.HBM,
    )
    half = exchange(picked.reshape(NC, NQ, 8, FD), CORE)
    gain = jnp.pad(draft_gain, (0, L - CW))[None]
    side = call(hidden_kernel, struct((2 * NQ, FD), BF), hidden, hidden_gain[None], proj_hidden.T, gain)
    sent = call(
        send_kernel,
        struct((NQ, 8, FD), BF),
        half,
        side,
        scratch=[pltpu.VMEM((NQ, 8, FD), BF), pltpu.SemaphoreType.DMA((NQ // 8,))],
        space=pltpu.HBM,
    )
    unit = call(unit_kernel, struct((NX, 24, FD), BF), exchange(sent, XY))
    got = lax.all_gather(exchange(unit, XS), "vocab", axis_index_groups=CORE)

    main_in = (hidden.astype(F32) * final_gain).astype(BF)
    main_part = jnp.dot(main_in, head_weight, preferred_element_type=F32)
    main = lax.psum_scatter(main_part, "dp", scatter_dimension=0, tiled=True)

    partial = call(
        proj_kernel,
        struct((NY, ZROWS, L), BF),
        got,
        hidden,
        embed_gain[None],
        weights,
        scratch=[pltpu.VMEM((RB * 8, L), F32)],
    )
    joined = call(join_kernel, struct((NQ, RB, L), BF), lax.all_to_all(partial, "dp", 0, 0))
    rows = lax.all_gather(exchange(joined, XY), "vocab", axis_index_groups=CORE)
    blocks = call(
        head_kernel,
        struct((NZ, HROWS, L), BF),
        rows,
        head_weight,
        scratch=[pltpu.VMEM((ROWS, FD), BF)],
    )
    parts = lax.all_to_all(blocks, "dp", 0, 0)
    main_logits, main_stats = call(main_kernel, (struct((RB, VD), F32), struct((8, L), F32)), rows, main)
    draft_logits, stats = call(
        stats_kernel, (struct((RB, VD), F32), struct((NQ * NC, 8, L), F32)), parts, main_stats
    )
    stats = lax.all_to_all(stats, "vocab", 0, 0)
    main_logp, draft_logp = call(
        final_kernel, (struct((RB, VD), BF), struct((RB, VD), BF)), stats, main_logits, draft_logits
    )
    return (main_logp, draft_logp)


def solution(mesh):
    return jax.shard_map(
        per_device,
        mesh=mesh,
        in_specs=(
            P(None, "dp"),
            P(),
            P("dp"),
            P("dp"),
            P("dp"),
            P("vocab", "dp"),
            P("dp", "vocab"),
            P("dp", "vocab"),
            P("vocab"),
            P("dp", "vocab"),
        ),
        out_specs=(P("dp", "vocab"), P("dp", "vocab")),
        check_vma=False,
    )
```

```python
import jax
import jax.numpy as jnp
from jax import lax
from jax.experimental import pallas as pl
from jax.experimental.pallas import tpu as pltpu
from jax.sharding import PartitionSpec as P

EPS = 1e-06
BF, F32 = jnp.bfloat16, jnp.float32
ROWS, D, V = 384, 7168, 65536
NZ, NY, NX, NC = 8, 8, 4, 2
NQ = NY * NX
FD = D // NZ
VD = V // (NQ * NC)
CW = D // (NQ * NC)
RB = ROWS // NZ
HB = RB // NC
L = 128
ZROWS = 2 * RB + 16
HROWS = RB * (VD // L) + 8
PARAMS = pltpu.CompilerParams(vmem_limit_bytes=48 * 1024 * 1024)


def vid(y, x, c):
    return (y * NX + x) * NC + c


CORE = [[vid(y, x, c) for c in range(NC)] for y in range(NY) for x in range(NX)]
YS = [[vid(y, x, c) for y in range(NY)] for x in range(NX) for c in range(NC)]
XY = [[vid(y, x, c) for y in range(NY) for x in range(NX)] for c in range(NC)]
XS = [[vid(y, x, c) for x in range(NX)] for y in range(NY) for c in range(NC)]


def iota(shape, dim):
    return lax.broadcasted_iota(jnp.int32, shape, dim)


def split(x):
    hi = x.astype(BF).astype(F32)
    return hi, x - hi


def ones(mask):
    return mask.astype(F32).astype(BF)


def dot(a, b):
    return jnp.dot(a, b, preferred_element_type=F32)


def dot_nt(a, b):
    return lax.dot_general(a, b, (((1,), (1,)), ((), ())), preferred_element_type=F32)


def place(rows, shape):
    row = iota(shape, 0)
    out = jnp.zeros(shape, F32)
    for k, v in enumerate(rows):
        out = jnp.where(row == k, v, out)
    return out


def call(kernel, outs, *args, scratch=(), space=pltpu.VMEM):
    single = not isinstance(outs, (list, tuple))
    shapes = [outs] if single else list(outs)
    specs = [pl.BlockSpec(memory_space=space) for _ in shapes]
    return pl.pallas_call(
        kernel,
        out_shape=shapes[0] if single else shapes,
        in_specs=[pl.BlockSpec(memory_space=pltpu.VMEM)] * len(args),
        out_specs=specs[0] if single else specs,
        scratch_shapes=list(scratch),
        compiler_params=PARAMS,
    )(*args)


def struct(shape, dtype):
    return jax.ShapeDtypeStruct(shape, dtype)


def pick_kernel(tokens, table, out, buf, sems):
    base = lax.axis_index("vocab") * VD
    tok = tokens[...].reshape(1, ROWS)
    part = iota((8, ROWS), 0)
    high = jnp.broadcast_to(tok >> 8, (8, ROWS)).astype(F32)
    low = jnp.broadcast_to(tok & 255, (8, ROWS)).astype(F32)
    codes = jnp.where(part == 0, high, jnp.where(part == 1, low, 0.0)).astype(BF)
    row = iota((ROWS, ROWS), 1)
    y, rest = row // RB, row % RB
    place_of = (rest // HB) * (NY * HB) + y * HB + rest % HB
    found = dot_nt(ones(iota((ROWS, ROWS), 0) == place_of), codes)
    local = (found[:, 0:1] * 256.0 + found[:, 1:2]).astype(jnp.int32) - base
    copies = []
    for start in range(0, ROWS, L):
        hot = ones(iota((L, VD), 1) == local[start : start + L])
        buf[start : start + L, :] = dot(hot, table[...]).astype(BF)
        part = pl.ds(start, L)
        copies.append(pltpu.make_async_copy(buf.at[part], out.at[part], sems.at[start // L]))
        copies[-1].start()
    for copy in copies:
        copy.wait()


def hidden_kernel(hidden, gain, ph, draft_gain, out):
    x = (hidden[...].astype(F32) * gain[...]).astype(BF)
    weights = jnp.concatenate([ph[...], jnp.zeros((L - CW, FD), BF)], axis=0)
    side = dot_nt(x, weights)
    last = place(split(draft_gain[...]), (8, L))
    for y in range(NY):
        tiles = [side[y * RB + i : y * RB + i + 8] for i in range(0, RB, 8)]
        out[y] = jnp.concatenate([*tiles, last], axis=1)


def send_kernel(half, side, out, buf, sems):
    copies = []
    for k in range(NY):
        rows = half[0, k].astype(F32) + half[1, k].astype(F32)
        buf[k] = jnp.concatenate([rows, side[k]], axis=0).astype(BF)
        if k % 2 == 1:
            part = pl.ds(k - 1, 2)
            copies.append(pltpu.make_async_copy(buf.at[part], out.at[part], sems.at[k // 2]))
            copies[-1].start()
    for copy in copies:
        copy.wait()


def unit_kernel(got, out):
    total = jnp.zeros((HB, FD), F32)
    for y in range(NY):
        total = total + got[y].astype(F32)[0:HB]
    out[...] = jnp.broadcast_to(total.astype(BF)[None], out.shape)


def proj_kernel(picked, lines, hidden, embed_gain, weights, out):
    y = lax.axis_index("vocab") // (NX * NC)
    h = hidden[pl.ds(pl.multiple_of(y * RB, 16), RB), :].astype(F32)
    halves = []
    for c in range(NC):
        half = picked[c, 0].astype(F32)
        for x in range(1, NX):
            half = half + picked[c, x].astype(F32)
        halves.append(half)
    e = jnp.concatenate(halves, axis=0)
    lane = iota((RB, L), 1)

    def extra(x):
        hi, low = split(jnp.sum(x * x, axis=1, keepdims=True))
        return jnp.where(lane == CW, hi, jnp.where(lane == CW + 1, low, 0.0))

    extra_h, extra_e = extra(h), extra(e)
    eg = (e * embed_gain[...]).astype(BF)
    pad = jnp.zeros((L - CW, FD), BF)
    for t in range(NY):
        w = jnp.concatenate([weights[t], pad], axis=0)
        block = lines[t].astype(F32)[HB : HB + 8]
        side = jnp.concatenate([block[:, i * L : (i + 1) * L] for i in range(RB // 8)], axis=0)
        gain = block[:, RB // 8 * L :]
        out[t, 0:RB, :] = (side + extra_h).astype(BF)
        out[t, RB : 2 * RB, :] = (dot_nt(eg, w) + extra_e).astype(BF)
        out[t, 2 * RB :, :] = place([gain[0:1], gain[1:2]], (16, L)).astype(BF)


def join_kernel(parts, out):
    total = parts[0].astype(F32)
    gain = jnp.sum(total[2 * RB :, :], axis=0, keepdims=True)
    for k in range(1, NZ):
        total = total + parts[k].astype(F32)
    lane = iota((RB, L), 1)
    sides = (lane == CW) | (lane == CW + 1)

    def scale(x):
        return lax.rsqrt(jnp.sum(jnp.where(sides, x, 0.0), axis=1, keepdims=True) / D + EPS)

    h, e = total[0:RB], total[RB : 2 * RB]
    inv_h = scale(h)
    projected = jnp.where(lane < CW, h * inv_h + e * scale(e), 0.0)
    sq_hi, sq_low = split(jnp.sum(projected * projected, axis=1, keepdims=True))
    h_hi, h_low = split(inv_h)
    x = projected * gain
    for k, v in enumerate((sq_hi, sq_low, h_hi, h_low)):
        x = jnp.where(lane == CW + k, v, x)
    out[...] = jnp.broadcast_to(x.astype(BF)[None], out.shape)


def head_kernel(rows, head, out, x_ref):
    squares = jnp.zeros((ROWS, L), F32)
    for x in range(NX):
        for c in range(NC):
            a = jnp.concatenate([rows[c, y * NX + x] for y in range(NY)], axis=0)
            j = x * NC + c
            x_ref[:, j * CW : (j + 1) * CW] = a[:, 0:CW]
            squares = squares + a.astype(F32)
    lane = iota((ROWS, L), 1)
    sq = jnp.sum(jnp.where((lane == CW) | (lane == CW + 1), squares, 0.0), axis=1, keepdims=True)
    diagonal = iota((RB, L), 0) == iota((RB, L), 1)
    part = iota((8, L), 0)
    for k in range(NZ):
        line = jnp.sum(jnp.where(diagonal, sq[k * RB : (k + 1) * RB], 0.0), axis=0, keepdims=True)
        out[k, HROWS - 8 :, :] = place(split(line), (8, L)).astype(BF)
    for n in range(0, VD, 256):
        acc = jnp.dot(x_ref[...], head[:, n : n + 256], preferred_element_type=F32).astype(BF)
        for m in range(2):
            tile = n // L + m
            for k in range(NZ):
                out[k, tile * RB : (tile + 1) * RB, :] = acc[k * RB : (k + 1) * RB, m * L : (m + 1) * L]


def summary(logits):
    diagonal = iota((RB, L), 0) == iota((RB, L), 1)
    top = jnp.max(logits, axis=1, keepdims=True)
    total = jnp.sum(jnp.exp(logits - top), axis=1, keepdims=True)
    return [jnp.sum(jnp.where(diagonal, v, 0.0), axis=0, keepdims=True) for v in (top, total)]


def main_kernel(rows, sums, out, stats):
    z = lax.axis_index("dp")
    lane = iota((RB, L), 1)
    block = rows[0, z * NX].astype(F32)
    scale = jnp.sum(jnp.where((lane == CW + 2) | (lane == CW + 3), block, 0.0), axis=1, keepdims=True)
    logits = sums[...] * scale
    out[...] = logits
    stats[...] = place(summary(logits), (8, L))


def stats_kernel(parts, main_stats, out, stats):
    diagonal = iota((RB, L), 0) == iota((RB, L), 1)
    tail = parts[0, HROWS - 8 :, :].astype(F32)
    for k in range(1, NZ):
        tail = tail + parts[k, HROWS - 8 :, :].astype(F32)
    squares = jnp.sum(jnp.where(diagonal, tail[0:1] + tail[1:2], 0.0), axis=1, keepdims=True)
    scale = lax.rsqrt(squares / D + EPS)
    for t in range(VD // L):
        acc = parts[0, t * RB : (t + 1) * RB, :].astype(F32)
        for k in range(1, NZ):
            acc = acc + parts[k, t * RB : (t + 1) * RB, :].astype(F32)
        out[:, t * L : (t + 1) * L] = acc * scale
    both = place([main_stats[0:1, :], main_stats[1:2, :], *summary(out[...])], (8, L))
    stats[...] = jnp.broadcast_to(both[None], stats.shape)


def final_kernel(stats, main, draft, main_out, draft_out):
    top = stats[0]
    for k in range(1, NQ * NC):
        top = jnp.maximum(top, stats[k])
    total = jnp.zeros((8, L), F32)
    for k in range(NQ * NC):
        total = total + stats[k] * pltpu.roll(jnp.exp(stats[k] - top), 1, 0)
    diagonal = iota((RB, L), 0) == iota((RB, L), 1)

    def column(line):
        return jnp.sum(jnp.where(diagonal, line, 0.0), axis=1, keepdims=True)

    for n, (logits, out) in enumerate(((main, main_out), (draft, draft_out))):
        shift = column(top[2 * n : 2 * n + 1])
        log_total = jnp.log(column(total[2 * n + 1 : 2 * n + 2]))
        out[...] = (logits[...] - shift - log_total).astype(BF)


def exchange(x, groups):
    return lax.all_to_all(x, "vocab", 0, 0, axis_index_groups=groups)


def per_device(
    hidden,
    tokens,
    final_gain,
    hidden_gain,
    embed_gain,
    embed_table,
    proj_hidden,
    proj_embed,
    draft_gain,
    head_weight,
):
    weights = lax.all_gather(proj_embed.T, "vocab", axis_index_groups=YS)

    picked = call(
        pick_kernel,
        struct((ROWS, FD), BF),
        tokens,
        embed_table,
        scratch=[pltpu.VMEM((ROWS, FD), BF), pltpu.SemaphoreType.DMA((ROWS // L,))],
        space=pltpu.HBM,
    )
    half = exchange(picked.reshape(NC, NY, HB, FD), CORE)
    gain = jnp.pad(draft_gain, (0, L - CW))[None]
    side = call(hidden_kernel, struct((NY, 8, FD), F32), hidden, hidden_gain[None], proj_hidden.T, gain)
    sent = call(
        send_kernel,
        struct((NY, HB + 8, FD), BF),
        half,
        side,
        scratch=[pltpu.VMEM((NY, HB + 8, FD), BF), pltpu.SemaphoreType.DMA((NY // 2,))],
        space=pltpu.HBM,
    )
    lines = exchange(sent, YS)
    unit = call(unit_kernel, struct((NX, HB, FD), BF), lines)
    got = lax.all_gather(exchange(unit, XS), "vocab", axis_index_groups=CORE)

    main_in = (hidden.astype(F32) * final_gain).astype(BF)
    main_part = jnp.dot(main_in, head_weight, preferred_element_type=F32)
    main = lax.psum_scatter(main_part, "dp", scatter_dimension=0, tiled=True)

    partial = call(
        proj_kernel,
        struct((NY, ZROWS, L), BF),
        got,
        lines,
        hidden,
        embed_gain[None],
        weights,
    )
    joined = call(join_kernel, struct((NQ, RB, L), BF), lax.all_to_all(partial, "dp", 0, 0))
    rows = lax.all_gather(exchange(joined, XY), "vocab", axis_index_groups=CORE)
    blocks = call(
        head_kernel,
        struct((NZ, HROWS, L), BF),
        rows,
        head_weight,
        scratch=[pltpu.VMEM((ROWS, FD), BF)],
    )
    parts = lax.all_to_all(blocks, "dp", 0, 0)
    main_logits, main_stats = call(main_kernel, (struct((RB, VD), F32), struct((8, L), F32)), rows, main)
    draft_logits, stats = call(
        stats_kernel, (struct((RB, VD), F32), struct((NQ * NC, 8, L), F32)), parts, main_stats
    )
    stats = lax.all_to_all(stats, "vocab", 0, 0)
    main_logp, draft_logp = call(
        final_kernel, (struct((RB, VD), BF), struct((RB, VD), BF)), stats, main_logits, draft_logits
    )
    return (main_logp, draft_logp)


def solution(mesh):
    return jax.shard_map(
        per_device,
        mesh=mesh,
        in_specs=(
            P(None, "dp"),
            P(),
            P("dp"),
            P("dp"),
            P("dp"),
            P("vocab", "dp"),
            P("dp", "vocab"),
            P("dp", "vocab"),
            P("vocab"),
            P("dp", "vocab"),
        ),
        out_specs=(P("dp", "vocab"), P("dp", "vocab")),
        check_vma=False,
    )
```

```python
import jax
import jax.numpy as jnp
from jax import lax
from jax.experimental import pallas as pl
from jax.experimental.pallas import tpu as pltpu
from jax.sharding import PartitionSpec as P

EPS = 1e-06
BF, F32 = jnp.bfloat16, jnp.float32
ROWS, D, V = 384, 7168, 65536
NZ, NY, NX, NC = 8, 8, 4, 2
NQ = NY * NX
FD = D // NZ
VD = V // (NQ * NC)
CW = D // (NQ * NC)
RB = ROWS // NZ
HB = RB // NC
L = 128
ZROWS = 2 * RB
HROWS = RB * (VD // L) + 16
PARAMS = pltpu.CompilerParams(vmem_limit_bytes=48 * 1024 * 1024)


def vid(y, x, c):
    return (y * NX + x) * NC + c


CORE = [[vid(y, x, c) for c in range(NC)] for y in range(NY) for x in range(NX)]
YS = [[vid(y, x, c) for y in range(NY)] for x in range(NX) for c in range(NC)]
XY = [[vid(y, x, c) for y in range(NY) for x in range(NX)] for c in range(NC)]
XS = [[vid(y, x, c) for x in range(NX)] for y in range(NY) for c in range(NC)]


def iota(shape, dim):
    return lax.broadcasted_iota(jnp.int32, shape, dim)


def split(x):
    hi = x.astype(BF).astype(F32)
    return hi, x - hi


def ones(mask):
    return mask.astype(F32).astype(BF)


def dot(a, b):
    return jnp.dot(a, b, preferred_element_type=F32)


def dot_nt(a, b):
    return lax.dot_general(a, b, (((1,), (1,)), ((), ())), preferred_element_type=F32)


def place(rows, shape):
    row = iota(shape, 0)
    out = jnp.zeros(shape, F32)
    for k, v in enumerate(rows):
        out = jnp.where(row == k, v, out)
    return out


def call(kernel, outs, *args, scratch=(), space=pltpu.VMEM):
    single = not isinstance(outs, (list, tuple))
    shapes = [outs] if single else list(outs)
    specs = [pl.BlockSpec(memory_space=space) for _ in shapes]
    return pl.pallas_call(
        kernel,
        out_shape=shapes[0] if single else shapes,
        in_specs=[pl.BlockSpec(memory_space=pltpu.VMEM)] * len(args),
        out_specs=specs[0] if single else specs,
        scratch_shapes=list(scratch),
        compiler_params=PARAMS,
    )(*args)


def struct(shape, dtype):
    return jax.ShapeDtypeStruct(shape, dtype)


def pick_kernel(tokens, table, out, buf, sems):
    base = lax.axis_index("vocab") * VD
    tok = tokens[...].reshape(1, ROWS)
    part = iota((8, ROWS), 0)
    high = jnp.broadcast_to(tok >> 8, (8, ROWS)).astype(F32)
    low = jnp.broadcast_to(tok & 255, (8, ROWS)).astype(F32)
    codes = jnp.where(part == 0, high, jnp.where(part == 1, low, 0.0)).astype(BF)
    row = iota((ROWS, ROWS), 1)
    y, rest = row // RB, row % RB
    place_of = (rest // HB) * (NY * HB) + y * HB + rest % HB
    found = dot_nt(ones(iota((ROWS, ROWS), 0) == place_of), codes)
    local = (found[:, 0:1] * 256.0 + found[:, 1:2]).astype(jnp.int32) - base
    copies = []
    for start in range(0, ROWS, L):
        hot = ones(iota((L, VD), 1) == local[start : start + L])
        buf[start : start + L, :] = dot(hot, table[...]).astype(BF)
        part = pl.ds(start, L)
        copies.append(pltpu.make_async_copy(buf.at[part], out.at[part], sems.at[start // L]))
        copies[-1].start()
    for copy in copies:
        copy.wait()


def hidden_kernel(hidden, gain, ph, draft_gain, out):
    x = (hidden[...].astype(F32) * gain[...]).astype(BF)
    weights = jnp.concatenate([ph[...], jnp.zeros((L - CW, FD), BF)], axis=0)
    side = dot_nt(x, weights)
    last = place(split(draft_gain[...]), (8, L))
    for y in range(NY):
        tiles = [side[y * RB + i : y * RB + i + 8] for i in range(0, RB, 8)]
        out[y] = jnp.concatenate([*tiles, last], axis=1)


def send_kernel(half, side, out, buf, sems):
    copies = []
    for k in range(NY):
        rows = half[0, k].astype(F32) + half[1, k].astype(F32)
        buf[k] = jnp.concatenate([rows, side[k]], axis=0).astype(BF)
        if k % 2 == 1:
            part = pl.ds(k - 1, 2)
            copies.append(pltpu.make_async_copy(buf.at[part], out.at[part], sems.at[k // 2]))
            copies[-1].start()
    for copy in copies:
        copy.wait()


def unit_kernel(got, out):
    total = jnp.zeros((HB, FD), F32)
    for y in range(NY):
        total = total + got[y].astype(F32)[0:HB]
    out[...] = jnp.broadcast_to(total.astype(BF)[None], out.shape)


def proj_kernel(picked, lines, hidden, embed_gain, weights, out):
    y = lax.axis_index("vocab") // (NX * NC)
    h = hidden[pl.ds(pl.multiple_of(y * RB, 16), RB), :].astype(F32)
    halves = []
    for c in range(NC):
        half = picked[c, 0].astype(F32)
        for x in range(1, NX):
            half = half + picked[c, x].astype(F32)
        halves.append(half)
    e = jnp.concatenate(halves, axis=0)
    lane = iota((RB, L), 1)

    def extra(x):
        hi, low = split(jnp.sum(x * x, axis=1, keepdims=True))
        return jnp.where(lane == CW, hi, jnp.where(lane == CW + 1, low, 0.0))

    extra_h, extra_e = extra(h), extra(e)
    eg = (e * embed_gain[...]).astype(BF)
    pad = jnp.zeros((L - CW, FD), BF)
    for t in range(NY):
        w = jnp.concatenate([weights[t], pad], axis=0)
        block = lines[t].astype(F32)[HB : HB + 8]
        side = jnp.concatenate([block[:, i * L : (i + 1) * L] for i in range(RB // 8)], axis=0)
        out[t, 0:RB, :] = (side + extra_h).astype(BF)
        out[t, RB : 2 * RB, :] = (dot_nt(eg, w) + extra_e).astype(BF)


def join_kernel(parts, lines, out):
    total = parts[0].astype(F32)
    gain = lines[lax.axis_index("dp")].astype(F32)[HB : HB + 2, RB // 8 * L :]
    gain = gain[0:1] + gain[1:2]
    for k in range(1, NZ):
        total = total + parts[k].astype(F32)
    lane = iota((RB, L), 1)
    sides = (lane == CW) | (lane == CW + 1)

    def scale(x):
        return lax.rsqrt(jnp.sum(jnp.where(sides, x, 0.0), axis=1, keepdims=True) / D + EPS)

    h, e = total[0:RB], total[RB : 2 * RB]
    inv_h = scale(h)
    projected = jnp.where(lane < CW, h * inv_h + e * scale(e), 0.0)
    sq_hi, sq_low = split(jnp.sum(projected * projected, axis=1, keepdims=True))
    h_hi, h_low = split(inv_h)
    x = projected * gain
    for k, v in enumerate((sq_hi, sq_low, h_hi, h_low)):
        x = jnp.where(lane == CW + k, v, x)
    out[...] = jnp.broadcast_to(x.astype(BF)[None], out.shape)


def head_kernel(rows, head, out, x_ref, buf, sems):
    squares = jnp.zeros((ROWS, L), F32)
    for x in range(NX):
        for c in range(NC):
            a = jnp.concatenate([rows[c, y * NX + x] for y in range(NY)], axis=0)
            j = x * NC + c
            x_ref[:, j * CW : (j + 1) * CW] = a[:, 0:CW]
            squares = squares + a.astype(F32)
    lane = iota((ROWS, L), 1)
    sq = jnp.sum(jnp.where((lane == CW) | (lane == CW + 1), squares, 0.0), axis=1, keepdims=True)
    diagonal = iota((RB, L), 0) == iota((RB, L), 1)
    for k in range(NZ):
        line = jnp.sum(jnp.where(diagonal, sq[k * RB : (k + 1) * RB], 0.0), axis=0, keepdims=True)
        buf[k, HROWS - 16 :, :] = place(split(line), (16, L)).astype(BF)
    copies = []
    for n in range(0, VD, 256):
        acc = dot(x_ref[...], head[:, n : n + 256]).astype(BF)
        first, last = n // L * RB, (n // L + 2) * RB
        for m in range(2):
            for k in range(NZ):
                at = first + m * RB
                buf[k, at : at + RB, :] = acc[k * RB : (k + 1) * RB, m * L : (m + 1) * L]
        part = pl.ds(first, (last if n + 256 < VD else HROWS) - first)
        copies.append(pltpu.make_async_copy(buf.at[:, part, :], out.at[:, part, :], sems.at[n // 256]))
        copies[-1].start()
    for copy in copies:
        copy.wait()


def summary(logits):
    diagonal = iota((RB, L), 0) == iota((RB, L), 1)
    top = jnp.max(logits, axis=1, keepdims=True)
    total = jnp.sum(jnp.exp(logits - top), axis=1, keepdims=True)
    return [jnp.sum(jnp.where(diagonal, v, 0.0), axis=0, keepdims=True) for v in (top, total)]


def main_kernel(rows, sums, out, stats):
    z = lax.axis_index("dp")
    lane = iota((RB, L), 1)
    block = rows[0, z * NX].astype(F32)
    scale = jnp.sum(jnp.where((lane == CW + 2) | (lane == CW + 3), block, 0.0), axis=1, keepdims=True)
    logits = sums[...] * scale
    out[...] = logits
    stats[...] = place(summary(logits), (8, L))


def stats_kernel(parts, main_stats, out, stats):
    diagonal = iota((RB, L), 0) == iota((RB, L), 1)
    tail = parts[0, HROWS - 16 :, :].astype(F32)
    for k in range(1, NZ):
        tail = tail + parts[k, HROWS - 16 :, :].astype(F32)
    squares = jnp.sum(jnp.where(diagonal, tail[0:1] + tail[1:2], 0.0), axis=1, keepdims=True)
    scale = lax.rsqrt(squares / D + EPS)
    for t in range(VD // L):
        acc = parts[0, t * RB : (t + 1) * RB, :].astype(F32)
        for k in range(1, NZ):
            acc = acc + parts[k, t * RB : (t + 1) * RB, :].astype(F32)
        out[:, t * L : (t + 1) * L] = acc * scale
    both = place([main_stats[0:1, :], main_stats[1:2, :], *summary(out[...])], (8, L))
    stats[...] = jnp.broadcast_to(both[None], stats.shape)


def final_kernel(stats, main, draft, main_out, draft_out):
    top = stats[0]
    for k in range(1, NQ * NC):
        top = jnp.maximum(top, stats[k])
    total = jnp.zeros((8, L), F32)
    for k in range(NQ * NC):
        total = total + stats[k] * pltpu.roll(jnp.exp(stats[k] - top), 1, 0)
    diagonal = iota((RB, L), 0) == iota((RB, L), 1)

    def column(line):
        return jnp.sum(jnp.where(diagonal, line, 0.0), axis=1, keepdims=True)

    for n, (logits, out) in enumerate(((main, main_out), (draft, draft_out))):
        shift = column(top[2 * n : 2 * n + 1])
        log_total = jnp.log(column(total[2 * n + 1 : 2 * n + 2]))
        out[...] = (logits[...] - shift - log_total).astype(BF)


def exchange(x, groups):
    return lax.all_to_all(x, "vocab", 0, 0, axis_index_groups=groups)


def per_device(
    hidden,
    tokens,
    final_gain,
    hidden_gain,
    embed_gain,
    embed_table,
    proj_hidden,
    proj_embed,
    draft_gain,
    head_weight,
):
    weights = lax.all_gather(proj_embed.T, "vocab", axis_index_groups=YS)

    picked = call(
        pick_kernel,
        struct((ROWS, FD), BF),
        tokens,
        embed_table,
        scratch=[pltpu.VMEM((ROWS, FD), BF), pltpu.SemaphoreType.DMA((ROWS // L,))],
        space=pltpu.HBM,
    )
    half = exchange(picked.reshape(NC, NY, HB, FD), CORE)
    gain = jnp.pad(draft_gain, (0, L - CW))[None]
    side = call(hidden_kernel, struct((NY, 8, FD), F32), hidden, hidden_gain[None], proj_hidden.T, gain)
    sent = call(
        send_kernel,
        struct((NY, HB + 8, FD), BF),
        half,
        side,
        scratch=[pltpu.VMEM((NY, HB + 8, FD), BF), pltpu.SemaphoreType.DMA((NY // 2,))],
        space=pltpu.HBM,
    )
    lines = exchange(sent, YS)
    unit = call(unit_kernel, struct((NX, HB, FD), BF), lines)
    got = lax.all_gather(exchange(unit, XS), "vocab", axis_index_groups=CORE)

    main_in = (hidden.astype(F32) * final_gain).astype(BF)
    main_part = jnp.dot(main_in, head_weight, preferred_element_type=F32)
    main = lax.psum_scatter(main_part, "dp", scatter_dimension=0, tiled=True)

    partial = call(
        proj_kernel,
        struct((NY, ZROWS, L), BF),
        got,
        lines,
        hidden,
        embed_gain[None],
        weights,
    )
    joined = call(join_kernel, struct((NQ, RB, L), BF), lax.all_to_all(partial, "dp", 0, 0), lines)
    rows = lax.all_gather(exchange(joined, XY), "vocab", axis_index_groups=CORE)
    blocks = call(
        head_kernel,
        struct((NZ, HROWS, L), BF),
        rows,
        head_weight,
        scratch=[
            pltpu.VMEM((ROWS, FD), BF),
            pltpu.VMEM((NZ, HROWS, L), BF),
            pltpu.SemaphoreType.DMA((VD // 256,)),
        ],
        space=pltpu.HBM,
    )
    parts = lax.all_to_all(blocks, "dp", 0, 0)
    main_logits, main_stats = call(main_kernel, (struct((RB, VD), F32), struct((8, L), F32)), rows, main)
    draft_logits, stats = call(
        stats_kernel, (struct((RB, VD), F32), struct((NQ * NC, 8, L), F32)), parts, main_stats
    )
    stats = lax.all_to_all(stats, "vocab", 0, 0)
    main_logp, draft_logp = call(
        final_kernel, (struct((RB, VD), BF), struct((RB, VD), BF)), stats, main_logits, draft_logits
    )
    return (main_logp, draft_logp)


def solution(mesh):
    return jax.shard_map(
        per_device,
        mesh=mesh,
        in_specs=(
            P(None, "dp"),
            P(),
            P("dp"),
            P("dp"),
            P("dp"),
            P("vocab", "dp"),
            P("dp", "vocab"),
            P("dp", "vocab"),
            P("vocab"),
            P("dp", "vocab"),
        ),
        out_specs=(P("dp", "vocab"), P("dp", "vocab")),
        check_vma=False,
    )
```

```python
import jax
import jax.numpy as jnp
from jax import lax
from jax.experimental import pallas as pl
from jax.experimental.pallas import tpu as pltpu
from jax.sharding import PartitionSpec as P

EPS = 1e-06
BF, F32 = jnp.bfloat16, jnp.float32
ROWS, D, V = 384, 7168, 65536
NZ, NY, NX, NC = 8, 8, 4, 2
NQ = NY * NX
FD = D // NZ
VD = V // (NQ * NC)
CW = D // (NQ * NC)
RB = ROWS // NZ
HB = RB // NC
L = 128
ZROWS = 2 * RB
HROWS = RB * (VD // L) + 16
PARAMS = pltpu.CompilerParams(vmem_limit_bytes=48 * 1024 * 1024)


def vid(y, x, c):
    return (y * NX + x) * NC + c


CORE = [[vid(y, x, c) for c in range(NC)] for y in range(NY) for x in range(NX)]
YS = [[vid(y, x, c) for y in range(NY)] for x in range(NX) for c in range(NC)]
XY = [[vid(y, x, c) for y in range(NY) for x in range(NX)] for c in range(NC)]
XS = [[vid(y, x, c) for x in range(NX)] for y in range(NY) for c in range(NC)]


def iota(shape, dim):
    return lax.broadcasted_iota(jnp.int32, shape, dim)


def split(x):
    hi = x.astype(BF).astype(F32)
    return hi, x - hi


def ones(mask):
    return mask.astype(F32).astype(BF)


def dot(a, b):
    return jnp.dot(a, b, preferred_element_type=F32)


def dot_nt(a, b):
    return lax.dot_general(a, b, (((1,), (1,)), ((), ())), preferred_element_type=F32)


def place(rows, shape):
    row = iota(shape, 0)
    out = jnp.zeros(shape, F32)
    for k, v in enumerate(rows):
        out = jnp.where(row == k, v, out)
    return out


def call(kernel, outs, *args, scratch=(), space=pltpu.VMEM):
    single = not isinstance(outs, (list, tuple))
    shapes = [outs] if single else list(outs)
    if space is pltpu.HBM:
        shapes = [pltpu.HBM(s.shape, s.dtype) for s in shapes]
    specs = [pl.BlockSpec(memory_space=space) for _ in shapes]
    return pl.pallas_call(
        kernel,
        out_shape=shapes[0] if single else shapes,
        in_specs=[pl.BlockSpec(memory_space=pltpu.VMEM)] * len(args),
        out_specs=specs[0] if single else specs,
        scratch_shapes=list(scratch),
        compiler_params=PARAMS,
    )(*args)


def struct(shape, dtype):
    return jax.ShapeDtypeStruct(shape, dtype)


def pick_kernel(tokens, table, out, buf, sems):
    base = lax.axis_index("vocab") * VD
    tok = tokens[...].reshape(1, ROWS)
    part = iota((8, ROWS), 0)
    high = jnp.broadcast_to(tok >> 8, (8, ROWS)).astype(F32)
    low = jnp.broadcast_to(tok & 255, (8, ROWS)).astype(F32)
    codes = jnp.where(part == 0, high, jnp.where(part == 1, low, 0.0)).astype(BF)
    row = iota((ROWS, ROWS), 1)
    y, rest = row // RB, row % RB
    place_of = (rest // HB) * (NY * HB) + y * HB + rest % HB
    found = dot_nt(ones(iota((ROWS, ROWS), 0) == place_of), codes)
    local = (found[:, 0:1] * 256.0 + found[:, 1:2]).astype(jnp.int32) - base
    copies = []
    for start in range(0, ROWS, L):
        hot = ones(iota((L, VD), 1) == local[start : start + L])
        buf[start : start + L, :] = dot(hot, table[...]).astype(BF)
        part = pl.ds(start, L)
        copies.append(pltpu.make_async_copy(buf.at[part], out.at[part], sems.at[start // L]))
        copies[-1].start()
    for copy in copies:
        copy.wait()


def hidden_kernel(hidden, gain, ph, draft_gain, out):
    x = (hidden[...].astype(F32) * gain[...]).astype(BF)
    weights = jnp.concatenate([ph[...], jnp.zeros((L - CW, FD), BF)], axis=0)
    side = dot_nt(x, weights)
    last = place(split(draft_gain[...]), (8, L))
    for y in range(NY):
        tiles = [side[y * RB + i : y * RB + i + 8] for i in range(0, RB, 8)]
        out[y] = jnp.concatenate([*tiles, last], axis=1)


def send_kernel(half, side, out, buf, sems):
    copies = []
    for k in range(NY):
        rows = half[0, k].astype(F32) + half[1, k].astype(F32)
        buf[k] = jnp.concatenate([rows, side[k]], axis=0).astype(BF)
        if k % 2 == 1:
            part = pl.ds(k - 1, 2)
            copies.append(pltpu.make_async_copy(buf.at[part], out.at[part], sems.at[k // 2]))
            copies[-1].start()
    for copy in copies:
        copy.wait()


def unit_kernel(got, out):
    total = jnp.zeros((HB, FD), F32)
    for y in range(NY):
        total = total + got[y].astype(F32)[0:HB]
    out[...] = jnp.broadcast_to(total.astype(BF)[None], out.shape)


def proj_kernel(picked, lines, hidden, embed_gain, weights, out):
    y = lax.axis_index("vocab") // (NX * NC)
    h = hidden[pl.ds(pl.multiple_of(y * RB, 16), RB), :].astype(F32)
    halves = []
    for c in range(NC):
        half = picked[c, 0].astype(F32)
        for x in range(1, NX):
            half = half + picked[c, x].astype(F32)
        halves.append(half)
    e = jnp.concatenate(halves, axis=0)
    lane = iota((RB, L), 1)

    def extra(x):
        hi, low = split(jnp.sum(x * x, axis=1, keepdims=True))
        return jnp.where(lane == CW, hi, jnp.where(lane == CW + 1, low, 0.0))

    extra_h, extra_e = extra(h), extra(e)
    eg = (e * embed_gain[...]).astype(BF)
    pad = jnp.zeros((L - CW, FD), BF)
    for t in range(NY):
        w = jnp.concatenate([weights[t], pad], axis=0)
        block = lines[t].astype(F32)[HB : HB + 8]
        side = jnp.concatenate([block[:, i * L : (i + 1) * L] for i in range(RB // 8)], axis=0)
        out[t, 0:RB, :] = (side + extra_h).astype(BF)
        out[t, RB : 2 * RB, :] = (dot_nt(eg, w) + extra_e).astype(BF)


def join_kernel(parts, lines, out):
    total = parts[0].astype(F32)
    gain = lines[lax.axis_index("dp")].astype(F32)[HB : HB + 2, RB // 8 * L :]
    gain = gain[0:1] + gain[1:2]
    for k in range(1, NZ):
        total = total + parts[k].astype(F32)
    lane = iota((RB, L), 1)
    sides = (lane == CW) | (lane == CW + 1)

    def scale(x):
        return lax.rsqrt(jnp.sum(jnp.where(sides, x, 0.0), axis=1, keepdims=True) / D + EPS)

    h, e = total[0:RB], total[RB : 2 * RB]
    inv_h = scale(h)
    projected = jnp.where(lane < CW, h * inv_h + e * scale(e), 0.0)
    sq_hi, sq_low = split(jnp.sum(projected * projected, axis=1, keepdims=True))
    h_hi, h_low = split(inv_h)
    x = projected * gain
    for k, v in enumerate((sq_hi, sq_low, h_hi, h_low)):
        x = jnp.where(lane == CW + k, v, x)
    out[...] = jnp.broadcast_to(x.astype(BF)[None], out.shape)


def pad_kernel(head, out):
    for j in range(NX * NC):
        out[j * L : j * L + CW, :] = head[j * CW : (j + 1) * CW, :]
        out[j * L + CW : (j + 1) * L, :] = jnp.zeros((L - CW, VD), BF)


def head_kernel(rows, head, out, x_ref, buf, sems):
    squares = jnp.zeros((ROWS, L), F32)
    for x in range(NX):
        for c in range(NC):
            j = x * NC + c
            for y in range(NY):
                x_ref[y * RB : (y + 1) * RB, j * L : (j + 1) * L] = rows[c, y * NX + x]
            squares = squares + x_ref[:, j * L : (j + 1) * L].astype(F32)
    lane = iota((ROWS, L), 1)
    sq = jnp.sum(jnp.where((lane == CW) | (lane == CW + 1), squares, 0.0), axis=1, keepdims=True)
    diagonal = iota((RB, L), 0) == iota((RB, L), 1)
    for k in range(NZ):
        line = jnp.sum(jnp.where(diagonal, sq[k * RB : (k + 1) * RB], 0.0), axis=0, keepdims=True)
        buf[k, HROWS - 16 :, :] = place(split(line), (16, L)).astype(BF)
    copies = []
    for n in range(0, VD, 256):
        acc = dot(x_ref[...], head[:, n : n + 256]).astype(BF)
        first, last = n // L * RB, (n // L + 2) * RB
        for m in range(2):
            for k in range(NZ):
                at = first + m * RB
                buf[k, at : at + RB, :] = acc[k * RB : (k + 1) * RB, m * L : (m + 1) * L]
        part = pl.ds(first, (last if n + 256 < VD else HROWS) - first)
        copies.append(pltpu.make_async_copy(buf.at[:, part, :], out.at[:, part, :], sems.at[n // 256]))
        copies[-1].start()
    for copy in copies:
        copy.wait()


def summary(logits):
    diagonal = iota((RB, L), 0) == iota((RB, L), 1)
    top = jnp.max(logits, axis=1, keepdims=True)
    total = jnp.sum(jnp.exp(logits - top), axis=1, keepdims=True)
    return [jnp.sum(jnp.where(diagonal, v, 0.0), axis=0, keepdims=True) for v in (top, total)]


def main_kernel(rows, sums, out, stats):
    z = lax.axis_index("dp")
    lane = iota((RB, L), 1)
    block = rows[0, z * NX].astype(F32)
    scale = jnp.sum(jnp.where((lane == CW + 2) | (lane == CW + 3), block, 0.0), axis=1, keepdims=True)
    logits = sums[...] * scale
    out[...] = logits
    stats[...] = place(summary(logits), (8, L))


def stats_kernel(parts, main_stats, out, stats):
    diagonal = iota((RB, L), 0) == iota((RB, L), 1)
    tail = parts[0, HROWS - 16 :, :].astype(F32)
    for k in range(1, NZ):
        tail = tail + parts[k, HROWS - 16 :, :].astype(F32)
    squares = jnp.sum(jnp.where(diagonal, tail[0:1] + tail[1:2], 0.0), axis=1, keepdims=True)
    scale = lax.rsqrt(squares / D + EPS)
    for t in range(VD // L):
        acc = parts[0, t * RB : (t + 1) * RB, :].astype(F32)
        for k in range(1, NZ):
            acc = acc + parts[k, t * RB : (t + 1) * RB, :].astype(F32)
        out[:, t * L : (t + 1) * L] = acc * scale
    both = place([main_stats[0:1, :], main_stats[1:2, :], *summary(out[...])], (8, L))
    stats[...] = jnp.broadcast_to(both[None], stats.shape)


def final_kernel(stats, main, draft, main_out, draft_out):
    top = stats[0]
    for k in range(1, NQ * NC):
        top = jnp.maximum(top, stats[k])
    total = jnp.zeros((8, L), F32)
    for k in range(NQ * NC):
        total = total + stats[k] * pltpu.roll(jnp.exp(stats[k] - top), 1, 0)
    diagonal = iota((RB, L), 0) == iota((RB, L), 1)

    def column(line):
        return jnp.sum(jnp.where(diagonal, line, 0.0), axis=1, keepdims=True)

    for n, (logits, out) in enumerate(((main, main_out), (draft, draft_out))):
        shift = column(top[2 * n : 2 * n + 1])
        log_total = jnp.log(column(total[2 * n + 1 : 2 * n + 2]))
        out[...] = (logits[...] - shift - log_total).astype(BF)


def exchange(x, groups):
    return lax.all_to_all(x, "vocab", 0, 0, axis_index_groups=groups)


def per_device(
    hidden,
    tokens,
    final_gain,
    hidden_gain,
    embed_gain,
    embed_table,
    proj_hidden,
    proj_embed,
    draft_gain,
    head_weight,
):
    weights = lax.all_gather(proj_embed.T, "vocab", axis_index_groups=YS)

    picked = call(
        pick_kernel,
        struct((ROWS, FD), BF),
        tokens,
        embed_table,
        scratch=[pltpu.VMEM((ROWS, FD), BF), pltpu.SemaphoreType.DMA((ROWS // L,))],
        space=pltpu.HBM,
    )
    half = exchange(picked.reshape(NC, NY, HB, FD), CORE)
    gain = jnp.pad(draft_gain, (0, L - CW))[None]
    side = call(hidden_kernel, struct((NY, 8, FD), F32), hidden, hidden_gain[None], proj_hidden.T, gain)
    sent = call(
        send_kernel,
        struct((NY, HB + 8, FD), BF),
        half,
        side,
        scratch=[pltpu.VMEM((NY, HB + 8, FD), BF), pltpu.SemaphoreType.DMA((NY // 2,))],
        space=pltpu.HBM,
    )
    lines = exchange(sent, YS)
    unit = call(unit_kernel, struct((NX, HB, FD), BF), lines)
    got = lax.all_gather(exchange(unit, XS), "vocab", axis_index_groups=CORE)

    main_in = (hidden.astype(F32) * final_gain).astype(BF)
    main_part = jnp.dot(main_in, head_weight, preferred_element_type=F32)
    main = lax.psum_scatter(main_part, "dp", scatter_dimension=0, tiled=True)

    partial = call(
        proj_kernel,
        struct((NY, ZROWS, L), BF),
        got,
        lines,
        hidden,
        embed_gain[None],
        weights,
    )
    joined = call(join_kernel, struct((NQ, RB, L), BF), lax.all_to_all(partial, "dp", 0, 0), lines)
    rows = lax.all_gather(exchange(joined, XY), "vocab", axis_index_groups=CORE)
    padded = call(pad_kernel, struct((NX * NC * L, VD), BF), head_weight)
    blocks = call(
        head_kernel,
        struct((NZ, HROWS, L), BF),
        rows,
        padded,
        scratch=[
            pltpu.VMEM((ROWS, NX * NC * L), BF),
            pltpu.VMEM((NZ, HROWS, L), BF),
            pltpu.SemaphoreType.DMA((VD // 256,)),
        ],
        space=pltpu.HBM,
    )
    parts = lax.all_to_all(blocks, "dp", 0, 0)
    main_logits, main_stats = call(main_kernel, (struct((RB, VD), F32), struct((8, L), F32)), rows, main)
    draft_logits, stats = call(
        stats_kernel, (struct((RB, VD), F32), struct((NQ * NC, 8, L), F32)), parts, main_stats
    )
    stats = lax.all_to_all(stats, "vocab", 0, 0)
    main_logp, draft_logp = call(
        final_kernel, (struct((RB, VD), BF), struct((RB, VD), BF)), stats, main_logits, draft_logits
    )
    return (main_logp, draft_logp)


def solution(mesh):
    return jax.shard_map(
        per_device,
        mesh=mesh,
        in_specs=(
            P(None, "dp"),
            P(),
            P("dp"),
            P("dp"),
            P("dp"),
            P("vocab", "dp"),
            P("dp", "vocab"),
            P("dp", "vocab"),
            P("vocab"),
            P("dp", "vocab"),
        ),
        out_specs=(P("dp", "vocab"), P("dp", "vocab")),
        check_vma=False,
    )
```

```python
import jax
import jax.numpy as jnp
from jax import lax
from jax.experimental import pallas as pl
from jax.experimental.pallas import tpu as pltpu
from jax.sharding import PartitionSpec as P

EPS = 1e-06
BF, F32 = jnp.bfloat16, jnp.float32
ROWS, D, V = 384, 7168, 65536
NZ, NY, NX, NC = 8, 8, 4, 2
NQ = NY * NX
FD = D // NZ
VD = V // (NQ * NC)
CW = D // (NQ * NC)
RB = ROWS // NZ
HB = RB // NC
L = 128
ZROWS = 2 * RB
HROWS = RB * (VD // L) + 16
PARAMS = pltpu.CompilerParams(vmem_limit_bytes=48 * 1024 * 1024)


def vid(y, x, c):
    return (y * NX + x) * NC + c


CORE = [[vid(y, x, c) for c in range(NC)] for y in range(NY) for x in range(NX)]
YS = [[vid(y, x, c) for y in range(NY)] for x in range(NX) for c in range(NC)]
XY = [[vid(y, x, c) for y in range(NY) for x in range(NX)] for c in range(NC)]
XS = [[vid(y, x, c) for x in range(NX)] for y in range(NY) for c in range(NC)]


def iota(shape, dim):
    return lax.broadcasted_iota(jnp.int32, shape, dim)


def split(x):
    hi = x.astype(BF).astype(F32)
    return hi, x - hi


def ones(mask):
    return mask.astype(F32).astype(BF)


def dot(a, b):
    return jnp.dot(a, b, preferred_element_type=F32)


def dot_nt(a, b):
    return lax.dot_general(a, b, (((1,), (1,)), ((), ())), preferred_element_type=F32)


def place(rows, shape):
    row = iota(shape, 0)
    out = jnp.zeros(shape, F32)
    for k, v in enumerate(rows):
        out = jnp.where(row == k, v, out)
    return out


def call(kernel, outs, *args, scratch=(), space=pltpu.VMEM, far=()):
    args = [pltpu.with_memory_space_constraint(a, pltpu.HBM) if k in far else a for k, a in enumerate(args)]
    single = not isinstance(outs, (list, tuple))
    shapes = [outs] if single else list(outs)
    if space is pltpu.HBM:
        shapes = [pltpu.HBM(s.shape, s.dtype) for s in shapes]
    specs = [pl.BlockSpec(memory_space=space) for _ in shapes]
    return pl.pallas_call(
        kernel,
        out_shape=shapes[0] if single else shapes,
        in_specs=[pl.BlockSpec(memory_space=pltpu.HBM if k in far else pltpu.VMEM) for k in range(len(args))],
        out_specs=specs[0] if single else specs,
        scratch_shapes=list(scratch),
        compiler_params=PARAMS,
    )(*args)


def struct(shape, dtype):
    return jax.ShapeDtypeStruct(shape, dtype)


def pick_kernel(tokens, table, out, buf, sems):
    base = lax.axis_index("vocab") * VD
    tok = tokens[...].reshape(1, ROWS)
    part = iota((8, ROWS), 0)
    high = jnp.broadcast_to(tok >> 8, (8, ROWS)).astype(F32)
    low = jnp.broadcast_to(tok & 255, (8, ROWS)).astype(F32)
    codes = jnp.where(part == 0, high, jnp.where(part == 1, low, 0.0)).astype(BF)
    row = iota((ROWS, ROWS), 1)
    y, rest = row // RB, row % RB
    place_of = (rest // HB) * (NY * HB) + y * HB + rest % HB
    found = dot_nt(ones(iota((ROWS, ROWS), 0) == place_of), codes)
    local = (found[:, 0:1] * 256.0 + found[:, 1:2]).astype(jnp.int32) - base
    copies = []
    for start in range(0, ROWS, L):
        hot = ones(iota((L, VD), 1) == local[start : start + L])
        buf[start : start + L, :] = dot(hot, table[...]).astype(BF)
        part = pl.ds(start, L)
        copies.append(pltpu.make_async_copy(buf.at[part], out.at[part], sems.at[start // L]))
        copies[-1].start()
    for copy in copies:
        copy.wait()


def hidden_kernel(hidden, gain, ph, draft_gain, out):
    x = (hidden[...].astype(F32) * gain[...]).astype(BF)
    weights = jnp.concatenate([ph[...], jnp.zeros((L - CW, FD), BF)], axis=0)
    side = dot_nt(x, weights)
    last = place(split(draft_gain[...]), (8, L))
    for y in range(NY):
        tiles = [side[y * RB + i : y * RB + i + 8] for i in range(0, RB, 8)]
        out[y] = jnp.concatenate([*tiles, last], axis=1)


def send_kernel(half, side, out, buf, sems):
    copies = []
    for k in range(NY):
        rows = half[0, k].astype(F32) + half[1, k].astype(F32)
        buf[k] = jnp.concatenate([rows, side[k]], axis=0).astype(BF)
        if k % 2 == 1:
            part = pl.ds(k - 1, 2)
            copies.append(pltpu.make_async_copy(buf.at[part], out.at[part], sems.at[k // 2]))
            copies[-1].start()
    for copy in copies:
        copy.wait()


def unit_kernel(got, out):
    total = jnp.zeros((HB, FD), F32)
    for y in range(NY):
        total = total + got[y].astype(F32)[0:HB]
    out[...] = jnp.broadcast_to(total.astype(BF)[None], out.shape)


def proj_kernel(picked, lines, hidden, embed_gain, weights, out, weights_v, sems):
    copies = [pltpu.make_async_copy(weights.at[t], weights_v.at[t], sems.at[t]) for t in range(NY)]
    for copy in copies:
        copy.start()
    y = lax.axis_index("vocab") // (NX * NC)
    h = hidden[pl.ds(pl.multiple_of(y * RB, 16), RB), :].astype(F32)
    halves = []
    for c in range(NC):
        half = picked[c, 0].astype(F32)
        for x in range(1, NX):
            half = half + picked[c, x].astype(F32)
        halves.append(half)
    e = jnp.concatenate(halves, axis=0)
    lane = iota((RB, L), 1)

    def extra(x):
        hi, low = split(jnp.sum(x * x, axis=1, keepdims=True))
        return jnp.where(lane == CW, hi, jnp.where(lane == CW + 1, low, 0.0))

    extra_h, extra_e = extra(h), extra(e)
    eg = (e * embed_gain[...].reshape(1, FD)).astype(BF)
    pad = jnp.zeros((L - CW, FD), BF)
    for t in range(NY):
        copies[t].wait()
        w = jnp.concatenate([weights_v[t], pad], axis=0)
        block = lines[t].astype(F32)[HB : HB + 8]
        side = jnp.concatenate([block[:, i * L : (i + 1) * L] for i in range(RB // 8)], axis=0)
        out[t, 0:RB, :] = (side + extra_h).astype(BF)
        out[t, RB : 2 * RB, :] = (dot_nt(eg, w) + extra_e).astype(BF)


def join_kernel(parts, lines, out):
    total = parts[0].astype(F32)
    gain = lines[lax.axis_index("dp")].astype(F32)[HB : HB + 2, RB // 8 * L :]
    gain = gain[0:1] + gain[1:2]
    for k in range(1, NZ):
        total = total + parts[k].astype(F32)
    lane = iota((RB, L), 1)
    sides = (lane == CW) | (lane == CW + 1)

    def scale(x):
        return lax.rsqrt(jnp.sum(jnp.where(sides, x, 0.0), axis=1, keepdims=True) / D + EPS)

    h, e = total[0:RB], total[RB : 2 * RB]
    inv_h = scale(h)
    projected = jnp.where(lane < CW, h * inv_h + e * scale(e), 0.0)
    sq_hi, sq_low = split(jnp.sum(projected * projected, axis=1, keepdims=True))
    h_hi, h_low = split(inv_h)
    x = projected * gain
    for k, v in enumerate((sq_hi, sq_low, h_hi, h_low)):
        x = jnp.where(lane == CW + k, v, x)
    out[...] = jnp.broadcast_to(x.astype(BF)[None], out.shape)


def head_kernel(rows, head, out, x_ref, buf, sems):
    squares = jnp.zeros((ROWS, L), F32)
    for x in range(NX):
        for c in range(NC):
            a = jnp.concatenate([rows[c, y * NX + x] for y in range(NY)], axis=0)
            j = x * NC + c
            x_ref[:, j * CW : (j + 1) * CW] = a[:, 0:CW]
            squares = squares + a.astype(F32)
    lane = iota((ROWS, L), 1)
    sq = jnp.sum(jnp.where((lane == CW) | (lane == CW + 1), squares, 0.0), axis=1, keepdims=True)
    diagonal = iota((RB, L), 0) == iota((RB, L), 1)
    for k in range(NZ):
        line = jnp.sum(jnp.where(diagonal, sq[k * RB : (k + 1) * RB], 0.0), axis=0, keepdims=True)
        buf[k, HROWS - 16 :, :] = place(split(line), (16, L)).astype(BF)
    copies = []
    for n in range(0, VD, 256):
        acc = dot(x_ref[...], head[:, n : n + 256]).astype(BF)
        first, last = n // L * RB, (n // L + 2) * RB
        for m in range(2):
            for k in range(NZ):
                at = first + m * RB
                buf[k, at : at + RB, :] = acc[k * RB : (k + 1) * RB, m * L : (m + 1) * L]
        part = pl.ds(first, (last if n + 256 < VD else HROWS) - first)
        copies.append(pltpu.make_async_copy(buf.at[:, part, :], out.at[:, part, :], sems.at[n // 256]))
        copies[-1].start()
    for copy in copies:
        copy.wait()


def summary(logits):
    diagonal = iota((RB, L), 0) == iota((RB, L), 1)
    top = jnp.max(logits, axis=1, keepdims=True)
    total = jnp.sum(jnp.exp(logits - top), axis=1, keepdims=True)
    return [jnp.sum(jnp.where(diagonal, v, 0.0), axis=0, keepdims=True) for v in (top, total)]


def main_kernel(rows, sums, out, stats):
    z = lax.axis_index("dp")
    lane = iota((RB, L), 1)
    block = rows[0, z * NX].astype(F32)
    scale = jnp.sum(jnp.where((lane == CW + 2) | (lane == CW + 3), block, 0.0), axis=1, keepdims=True)
    logits = sums[...] * scale
    out[...] = logits
    stats[...] = place(summary(logits), (8, L))


def stats_kernel(parts, main_stats, out, stats):
    diagonal = iota((RB, L), 0) == iota((RB, L), 1)
    tail = parts[0, HROWS - 16 :, :].astype(F32)
    for k in range(1, NZ):
        tail = tail + parts[k, HROWS - 16 :, :].astype(F32)
    squares = jnp.sum(jnp.where(diagonal, tail[0:1] + tail[1:2], 0.0), axis=1, keepdims=True)
    scale = lax.rsqrt(squares / D + EPS)
    for t in range(VD // L):
        acc = parts[0, t * RB : (t + 1) * RB, :].astype(F32)
        for k in range(1, NZ):
            acc = acc + parts[k, t * RB : (t + 1) * RB, :].astype(F32)
        out[:, t * L : (t + 1) * L] = acc * scale
    both = place([main_stats[0:1, :], main_stats[1:2, :], *summary(out[...])], (8, L))
    stats[...] = jnp.broadcast_to(both[None], stats.shape)


def final_kernel(stats, main, draft, main_out, draft_out):
    top = stats[0]
    for k in range(1, NQ * NC):
        top = jnp.maximum(top, stats[k])
    total = jnp.zeros((8, L), F32)
    for k in range(NQ * NC):
        total = total + stats[k] * pltpu.roll(jnp.exp(stats[k] - top), 1, 0)
    diagonal = iota((RB, L), 0) == iota((RB, L), 1)

    def column(line):
        return jnp.sum(jnp.where(diagonal, line, 0.0), axis=1, keepdims=True)

    for n, (logits, out) in enumerate(((main, main_out), (draft, draft_out))):
        shift = column(top[2 * n : 2 * n + 1])
        log_total = jnp.log(column(total[2 * n + 1 : 2 * n + 2]))
        out[...] = (logits[...] - shift - log_total).astype(BF)


def exchange(x, groups):
    return lax.all_to_all(x, "vocab", 0, 0, axis_index_groups=groups)


def per_device(
    hidden,
    tokens,
    final_gain,
    hidden_gain,
    embed_gain,
    embed_table,
    proj_hidden,
    proj_embed,
    draft_gain,
    head_weight,
):
    weights = lax.all_gather(proj_embed.T, "vocab", axis_index_groups=YS)

    picked = call(
        pick_kernel,
        struct((ROWS, FD), BF),
        tokens,
        embed_table,
        scratch=[pltpu.VMEM((ROWS, FD), BF), pltpu.SemaphoreType.DMA((ROWS // L,))],
        space=pltpu.HBM,
    )
    half = exchange(picked.reshape(NC, NY, HB, FD), CORE)
    gain = jnp.pad(draft_gain, (0, L - CW))[None]
    side = call(hidden_kernel, struct((NY, 8, FD), F32), hidden, hidden_gain[None], proj_hidden.T, gain)
    sent = call(
        send_kernel,
        struct((NY, HB + 8, FD), BF),
        half,
        side,
        scratch=[pltpu.VMEM((NY, HB + 8, FD), BF), pltpu.SemaphoreType.DMA((NY // 2,))],
        space=pltpu.HBM,
    )
    lines = exchange(sent, YS)
    unit = call(unit_kernel, struct((NX, HB, FD), BF), lines)
    got = lax.all_gather(exchange(unit, XS), "vocab", axis_index_groups=CORE)

    main_in = (hidden.astype(F32) * final_gain).astype(BF)
    main_part = jnp.dot(main_in, head_weight, preferred_element_type=F32)
    main = lax.psum_scatter(main_part, "dp", scatter_dimension=0, tiled=True)

    partial = call(
        proj_kernel,
        struct((NY, ZROWS, L), BF),
        got,
        lines,
        hidden,
        embed_gain,
        weights,
        far=(4,),
        scratch=[pltpu.VMEM((NY, CW, FD), BF), pltpu.SemaphoreType.DMA((NY,))],
    )
    joined = call(join_kernel, struct((NQ, RB, L), BF), lax.all_to_all(partial, "dp", 0, 0), lines)
    rows = lax.all_gather(exchange(joined, XY), "vocab", axis_index_groups=CORE)
    blocks = call(
        head_kernel,
        struct((NZ, HROWS, L), BF),
        rows,
        head_weight,
        scratch=[
            pltpu.VMEM((ROWS, FD), BF),
            pltpu.VMEM((NZ, HROWS, L), BF),
            pltpu.SemaphoreType.DMA((VD // 256,)),
        ],
        space=pltpu.HBM,
    )
    parts = lax.all_to_all(blocks, "dp", 0, 0)
    main_logits, main_stats = call(main_kernel, (struct((RB, VD), F32), struct((8, L), F32)), rows, main)
    draft_logits, stats = call(
        stats_kernel, (struct((RB, VD), F32), struct((NQ * NC, 8, L), F32)), parts, main_stats
    )
    stats = lax.all_to_all(stats, "vocab", 0, 0)
    main_logp, draft_logp = call(
        final_kernel, (struct((RB, VD), BF), struct((RB, VD), BF)), stats, main_logits, draft_logits
    )
    return (main_logp, draft_logp)


def solution(mesh):
    return jax.shard_map(
        per_device,
        mesh=mesh,
        in_specs=(
            P(None, "dp"),
            P(),
            P("dp"),
            P("dp"),
            P("dp"),
            P("vocab", "dp"),
            P("dp", "vocab"),
            P("dp", "vocab"),
            P("vocab"),
            P("dp", "vocab"),
        ),
        out_specs=(P("dp", "vocab"), P("dp", "vocab")),
        check_vma=False,
    )
```

```python
import jax
import jax.numpy as jnp
from jax import lax
from jax.experimental import pallas as pl
from jax.experimental.pallas import tpu as pltpu
from jax.sharding import PartitionSpec as P

EPS = 1e-06
BF, F32 = jnp.bfloat16, jnp.float32
ROWS, D, V = 384, 7168, 65536
NZ, NY, NX, NC = 8, 8, 4, 2
NQ = NY * NX
FD = D // NZ
VD = V // (NQ * NC)
CW = D // (NQ * NC)
RB = ROWS // NZ
HB = RB // NC
L = 128
ZROWS = 2 * RB
HROWS = RB * (VD // L) + 16
PARAMS = pltpu.CompilerParams(vmem_limit_bytes=48 * 1024 * 1024)


def vid(y, x, c):
    return (y * NX + x) * NC + c


CORE = [[vid(y, x, c) for c in range(NC)] for y in range(NY) for x in range(NX)]
YS = [[vid(y, x, c) for y in range(NY)] for x in range(NX) for c in range(NC)]
XY = [[vid(y, x, c) for y in range(NY) for x in range(NX)] for c in range(NC)]
XS = [[vid(y, x, c) for x in range(NX)] for y in range(NY) for c in range(NC)]


def iota(shape, dim):
    return lax.broadcasted_iota(jnp.int32, shape, dim)


def split(x):
    hi = x.astype(BF).astype(F32)
    return hi, x - hi


def ones(mask):
    return mask.astype(F32).astype(BF)


def dot(a, b):
    return jnp.dot(a, b, preferred_element_type=F32)


def dot_nt(a, b):
    return lax.dot_general(a, b, (((1,), (1,)), ((), ())), preferred_element_type=F32)


def place(rows, shape):
    row = iota(shape, 0)
    out = jnp.zeros(shape, F32)
    for k, v in enumerate(rows):
        out = jnp.where(row == k, v, out)
    return out


def call(kernel, outs, *args, scratch=(), space=pltpu.VMEM):
    single = not isinstance(outs, (list, tuple))
    shapes = [outs] if single else list(outs)
    if space is pltpu.HBM:
        shapes = [pltpu.HBM(s.shape, s.dtype) for s in shapes]
    specs = [pl.BlockSpec(memory_space=space) for _ in shapes]
    return pl.pallas_call(
        kernel,
        out_shape=shapes[0] if single else shapes,
        in_specs=[pl.BlockSpec(memory_space=pltpu.VMEM)] * len(args),
        out_specs=specs[0] if single else specs,
        scratch_shapes=list(scratch),
        compiler_params=PARAMS,
    )(*args)


def struct(shape, dtype):
    return jax.ShapeDtypeStruct(shape, dtype)


def pick_kernel(tokens, table, out, buf, sems):
    base = lax.axis_index("vocab") * VD
    tok = tokens[...].reshape(1, ROWS)
    part = iota((8, ROWS), 0)
    high = jnp.broadcast_to(tok >> 8, (8, ROWS)).astype(F32)
    low = jnp.broadcast_to(tok & 255, (8, ROWS)).astype(F32)
    codes = jnp.where(part == 0, high, jnp.where(part == 1, low, 0.0)).astype(BF)
    row = iota((ROWS, ROWS), 1)
    y, rest = row // RB, row % RB
    place_of = (rest // HB) * (NY * HB) + y * HB + rest % HB
    found = dot_nt(ones(iota((ROWS, ROWS), 0) == place_of), codes)
    local = (found[:, 0:1] * 256.0 + found[:, 1:2]).astype(jnp.int32) - base
    copies = []
    for start in range(0, ROWS, L):
        hot = ones(iota((L, VD), 1) == local[start : start + L])
        buf[start : start + L, :] = dot(hot, table[...]).astype(BF)
        part = pl.ds(start, L)
        copies.append(pltpu.make_async_copy(buf.at[part], out.at[part], sems.at[start // L]))
        copies[-1].start()
    for copy in copies:
        copy.wait()


def hidden_kernel(hidden, gain, ph, draft_gain, out):
    x = (hidden[...].astype(F32) * gain[...]).astype(BF)
    weights = jnp.concatenate([ph[...], jnp.zeros((L - CW, FD), BF)], axis=0)
    side = dot_nt(x, weights)
    last = place(split(draft_gain[...]), (8, L))
    for y in range(NY):
        tiles = [side[y * RB + i : y * RB + i + 8] for i in range(0, RB, 8)]
        out[y] = jnp.concatenate([*tiles, last], axis=1)


def send_kernel(half, side, out, buf, sems):
    copies = []
    for k in range(NY):
        rows = half[0, k].astype(F32) + half[1, k].astype(F32)
        buf[k] = jnp.concatenate([rows, side[k]], axis=0).astype(BF)
        if k % 2 == 1:
            part = pl.ds(k - 1, 2)
            copies.append(pltpu.make_async_copy(buf.at[part], out.at[part], sems.at[k // 2]))
            copies[-1].start()
    for copy in copies:
        copy.wait()


def unit_kernel(got, out):
    total = jnp.zeros((HB, FD), F32)
    for y in range(NY):
        total = total + got[y].astype(F32)[0:HB]
    out[...] = jnp.broadcast_to(total.astype(BF)[None], out.shape)


def proj_kernel(picked, lines, hidden, embed_gain, weights, out):
    y = lax.axis_index("vocab") // (NX * NC)
    h = hidden[pl.ds(pl.multiple_of(y * RB, 16), RB), :].astype(F32)
    halves = []
    for c in range(NC):
        half = picked[c, 0].astype(F32)
        for x in range(1, NX):
            half = half + picked[c, x].astype(F32)
        halves.append(half)
    e = jnp.concatenate(halves, axis=0)
    lane = iota((RB, L), 1)

    def extra(x):
        hi, low = split(jnp.sum(x * x, axis=1, keepdims=True))
        return jnp.where(lane == CW, hi, jnp.where(lane == CW + 1, low, 0.0))

    extra_h, extra_e = extra(h), extra(e)
    eg = (e * embed_gain[...].reshape(1, FD)).astype(BF)
    pad = jnp.zeros((L - CW, FD), BF)
    for t in range(NY):
        w = jnp.concatenate([weights[t], pad], axis=0)
        block = lines[t].astype(F32)[HB : HB + 8]
        side = jnp.concatenate([block[:, i * L : (i + 1) * L] for i in range(RB // 8)], axis=0)
        out[t, 0:RB, :] = (side + extra_h).astype(BF)
        out[t, RB : 2 * RB, :] = (dot_nt(eg, w) + extra_e).astype(BF)


def join_kernel(parts, lines, out):
    total = parts[0].astype(F32)
    gain = lines[lax.axis_index("dp")].astype(F32)[HB : HB + 2, RB // 8 * L :]
    gain = gain[0:1] + gain[1:2]
    for k in range(1, NZ):
        total = total + parts[k].astype(F32)
    lane = iota((RB, L), 1)
    sides = (lane == CW) | (lane == CW + 1)

    def scale(x):
        return lax.rsqrt(jnp.sum(jnp.where(sides, x, 0.0), axis=1, keepdims=True) / D + EPS)

    h, e = total[0:RB], total[RB : 2 * RB]
    inv_h = scale(h)
    projected = jnp.where(lane < CW, h * inv_h + e * scale(e), 0.0)
    sq_hi, sq_low = split(jnp.sum(projected * projected, axis=1, keepdims=True))
    h_hi, h_low = split(inv_h)
    x = projected * gain
    for k, v in enumerate((sq_hi, sq_low, h_hi, h_low)):
        x = jnp.where(lane == CW + k, v, x)
    out[...] = jnp.broadcast_to(x.astype(BF)[None], out.shape)


def head_kernel(rows, head, out, x_ref, buf, sems):
    squares = jnp.zeros((ROWS, L), F32)
    for x in range(NX):
        for c in range(NC):
            a = jnp.concatenate([rows[c, y * NX + x] for y in range(NY)], axis=0)
            j = x * NC + c
            x_ref[:, j * CW : (j + 1) * CW] = a[:, 0:CW]
            squares = squares + a.astype(F32)
    lane = iota((ROWS, L), 1)
    sq = jnp.sum(jnp.where((lane == CW) | (lane == CW + 1), squares, 0.0), axis=1, keepdims=True)
    diagonal = iota((RB, L), 0) == iota((RB, L), 1)
    for k in range(NZ):
        line = jnp.sum(jnp.where(diagonal, sq[k * RB : (k + 1) * RB], 0.0), axis=0, keepdims=True)
        buf[k, HROWS - 16 :, :] = place(split(line), (16, L)).astype(BF)
    copies = []
    for n in range(0, VD, 256):
        acc = dot(x_ref[...], head[:, n : n + 256]).astype(BF)
        first, last = n // L * RB, (n // L + 2) * RB
        for m in range(2):
            for k in range(NZ):
                at = first + m * RB
                buf[k, at : at + RB, :] = acc[k * RB : (k + 1) * RB, m * L : (m + 1) * L]
        part = pl.ds(first, (last if n + 256 < VD else HROWS) - first)
        copies.append(pltpu.make_async_copy(buf.at[:, part, :], out.at[:, part, :], sems.at[n // 256]))
        copies[-1].start()
    for copy in copies:
        copy.wait()


def summary(logits):
    diagonal = iota((RB, L), 0) == iota((RB, L), 1)
    top = jnp.max(logits, axis=1, keepdims=True)
    total = jnp.sum(jnp.exp(logits - top), axis=1, keepdims=True)
    return [jnp.sum(jnp.where(diagonal, v, 0.0), axis=0, keepdims=True) for v in (top, total)]


def main_kernel(rows, sums, out, stats):
    z = lax.axis_index("dp")
    lane = iota((RB, L), 1)
    block = rows[0, z * NX].astype(F32)
    scale = jnp.sum(jnp.where((lane == CW + 2) | (lane == CW + 3), block, 0.0), axis=1, keepdims=True)
    logits = sums[...] * scale
    out[...] = logits
    stats[...] = place(summary(logits), (8, L))


def stats_kernel(parts, main_stats, out, stats):
    diagonal = iota((RB, L), 0) == iota((RB, L), 1)
    tail = parts[0, HROWS - 16 :, :].astype(F32)
    for k in range(1, NZ):
        tail = tail + parts[k, HROWS - 16 :, :].astype(F32)
    squares = jnp.sum(jnp.where(diagonal, tail[0:1] + tail[1:2], 0.0), axis=1, keepdims=True)
    scale = lax.rsqrt(squares / D + EPS)
    for t in range(VD // L):
        acc = parts[0, t * RB : (t + 1) * RB, :].astype(F32)
        for k in range(1, NZ):
            acc = acc + parts[k, t * RB : (t + 1) * RB, :].astype(F32)
        out[:, t * L : (t + 1) * L] = acc * scale
    both = place([main_stats[0:1, :], main_stats[1:2, :], *summary(out[...])], (8, L))
    stats[...] = jnp.broadcast_to(both[None], stats.shape)


def final_kernel(stats, main, draft, main_out, draft_out):
    top = stats[0]
    for k in range(1, NQ * NC):
        top = jnp.maximum(top, stats[k])
    total = jnp.zeros((8, L), F32)
    for k in range(NQ * NC):
        total = total + stats[k] * pltpu.roll(jnp.exp(stats[k] - top), 1, 0)
    diagonal = iota((RB, L), 0) == iota((RB, L), 1)

    def column(line):
        return jnp.sum(jnp.where(diagonal, line, 0.0), axis=1, keepdims=True)

    for n, (logits, out) in enumerate(((main, main_out), (draft, draft_out))):
        shift = column(top[2 * n : 2 * n + 1])
        log_total = jnp.log(column(total[2 * n + 1 : 2 * n + 2]))
        out[...] = (logits[...] - shift - log_total).astype(BF)


def exchange(x, groups):
    return lax.all_to_all(x, "vocab", 0, 0, axis_index_groups=groups)


def per_device(
    hidden,
    tokens,
    final_gain,
    hidden_gain,
    embed_gain,
    embed_table,
    proj_hidden,
    proj_embed,
    draft_gain,
    head_weight,
):
    weights = lax.all_gather(proj_embed.T, "vocab", axis_index_groups=YS)

    picked = call(
        pick_kernel,
        struct((ROWS, FD), BF),
        tokens,
        embed_table,
        scratch=[pltpu.VMEM((ROWS, FD), BF), pltpu.SemaphoreType.DMA((ROWS // L,))],
        space=pltpu.HBM,
    )
    half = exchange(picked.reshape(NC, NY, HB, FD), CORE)
    gain = jnp.pad(draft_gain, (0, L - CW))[None]
    side = call(hidden_kernel, struct((NY, 8, FD), F32), hidden, hidden_gain[None], proj_hidden.T, gain)
    sent = call(
        send_kernel,
        struct((NY, HB + 8, FD), BF),
        half,
        side,
        scratch=[pltpu.VMEM((NY, HB + 8, FD), BF), pltpu.SemaphoreType.DMA((NY // 2,))],
        space=pltpu.HBM,
    )
    lines = exchange(sent, YS)
    unit = call(unit_kernel, struct((NX, HB, FD), BF), lines)
    got = lax.all_gather(exchange(unit, XS), "vocab", axis_index_groups=CORE)

    main_in = (hidden.astype(F32) * final_gain).astype(BF)
    main_part = jnp.dot(main_in, head_weight, preferred_element_type=F32)
    main = lax.psum_scatter(main_part, "dp", scatter_dimension=0, tiled=True)

    partial = call(
        proj_kernel,
        struct((NY, ZROWS, L), BF),
        got,
        lines,
        hidden,
        embed_gain,
        weights,
    )
    joined = call(join_kernel, struct((NQ, RB, L), BF), lax.all_to_all(partial, "dp", 0, 0), lines)
    rows = lax.all_gather(exchange(joined, XY), "vocab", axis_index_groups=CORE)
    blocks = call(
        head_kernel,
        struct((NZ, HROWS, L), BF),
        rows,
        head_weight,
        scratch=[
            pltpu.VMEM((ROWS, FD), BF),
            pltpu.VMEM((NZ, HROWS, L), BF),
            pltpu.SemaphoreType.DMA((VD // 256,)),
        ],
        space=pltpu.HBM,
    )
    parts = lax.all_to_all(blocks, "dp", 0, 0)
    main_logits, main_stats = call(main_kernel, (struct((RB, VD), F32), struct((8, L), F32)), rows, main)
    draft_logits, stats = call(
        stats_kernel, (struct((RB, VD), F32), struct((NQ * NC, 8, L), F32)), parts, main_stats
    )
    stats = lax.all_to_all(stats, "vocab", 0, 0)
    main_logp, draft_logp = call(
        final_kernel, (struct((RB, VD), BF), struct((RB, VD), BF)), stats, main_logits, draft_logits
    )
    return (main_logp, draft_logp)


def solution(mesh):
    return jax.shard_map(
        per_device,
        mesh=mesh,
        in_specs=(
            P(None, "dp"),
            P(),
            P("dp"),
            P("dp"),
            P("dp"),
            P("vocab", "dp"),
            P("dp", "vocab"),
            P("dp", "vocab"),
            P("vocab"),
            P("dp", "vocab"),
        ),
        out_specs=(P("dp", "vocab"), P("dp", "vocab")),
        check_vma=False,
    )
```
